32 devices in a mesh: seq: 4 (over y, core), fsdp: 8 (over z, x).
Axes of the slice: x: 2, y: 2, z: 4, core: 2. Of those that a mesh axis runs over, the one named last changes fastest.
Arguments:
- tokens: bfloat16 [8, 1024, 2048], P('fsdp', 'seq'), may hold values from -6 to 6
- gain_attn: bfloat16 [2048], P('fsdp'), may hold values from 0.5 to 1.5
- w_qkv: bfloat16 [2048, 2560], P('fsdp'), may hold values from -0.125 to 0.125
- w_out: bfloat16 [2048, 2048], P('fsdp'), may hold values from -3 to 3
- gain_mlp: bfloat16 [2048], P('fsdp'), may hold values from 0.5 to 1.5
- w_gate_up: bfloat16 [2048, 11264], P('fsdp'), may hold values from -0.125 to 0.125
- w_down: bfloat16 [2048, 5632], P('fsdp'), may hold values from -0.078125 to 0.078125
- cotangent: bfloat16 [8, 1024, 2048], P('fsdp', 'seq'), may hold values from -6 to 6
Outputs:
- output: bfloat16 [8, 1024, 2048], P('fsdp', 'seq')
- grad_tokens: float32 [8, 1024, 2048], P('fsdp', 'seq')
- grad_w_qkv: float32 [2048, 2560], P('fsdp')
- grad_w_out: float32 [2048, 2048], P('fsdp')
- grad_w_gate_up: float32 [2048, 11264], P('fsdp')
- grad_w_down: float32 [2048, 5632], P('fsdp')
- grad_gain_attn: float32 [2048], P('fsdp')
- grad_gain_mlp: float32 [2048], P('fsdp')
The draws below stay inside these ranges and needn't reach their ends.
All inputs are finite; a program needn't handle non-finite values.
Results may differ from the reference program's by a relative error of at most 0.02.
Values may be sent and summed in bfloat16 or wider, within the bound.
No kernel may reach another device: no remote copies, remote signals or barrier semaphores. Data moves between devices by JAX's collectives and lax.ppermute only.
A program may use at most 576 MiB of HBM per device.

```python
import jax
import jax.numpy as jnp
from jax import lax

D = 2048
H = 32
KVH = 4
HDIM = 64
FF = 5632
SEQ_LEN = 8192
SLAB = 1024
BLOCKS = 8
SEQS = 1


def raised(values, rng, source, target, shards_of, factor):
    def block_of(position):
        return (jnp.arange(values.shape[position]) // (values.shape[position] // shards_of)).reshape((-1,) + (1,) * (values.ndim - 1 - position))

    first = jax.random.permutation(rng, shards_of)[block_of(target)]
    second = (block_of(target) + shards_of // 2) % shards_of
    return jnp.where((block_of(source) == first) | (block_of(source) == second), factor * values, values)


def steps_of(key, extent, split, smallest, largest):
    factor_of, own = 1.0, jax.random.fold_in(key, 6)
    for dim, shards_of in split:
        heights = jnp.exp(jax.random.uniform(jax.random.fold_in(own, dim), (shards_of,), jnp.float32, smallest / len(split), largest / len(split)))
        factor_of = factor_of * jnp.repeat(heights, extent[dim] // shards_of).reshape([-1 if axis == dim else 1 for axis in range(len(extent))])
    return factor_of


def centred(rng, dims, scale, reach, split=(), kind=jnp.bfloat16):
    level = steps_of(rng, dims, split, -0.22, 0.18) if split else 1.0
    values = jax.random.normal(rng, dims, jnp.float32) * scale * level
    return jnp.minimum(jnp.maximum(values, -reach), reach).astype(kind)


def heavy_noise(key, shape, scale, bound, shards, heavy, held_as=jnp.bfloat16):
    drawn = scale * jax.random.normal(key, shape, jnp.float32)
    if shards:
        drawn = drawn * steps_of(key, shape, shards, -0.22, 0.18)
    return jnp.clip(raised(drawn, jax.random.fold_in(key, 3), *heavy), -bound, bound).astype(held_as)


def setup_inputs(seed: int = 0) -> dict:
    seeds = jax.random.split(jax.random.key(seed), 9)
    return {
        "tokens": heavy_noise(seeds[0], (BLOCKS, SLAB, D), 1.0, 6.0, ((0, 8), (1, 4)), (0, 2, 8, 2.0)),
        "gain_attn": jnp.clip(1.0 + 0.1 * jax.random.normal(seeds[1], (D,), jnp.float32), 0.5, 1.5).astype(jnp.bfloat16),
        "w_qkv": centred(seeds[2], (D, H * HDIM + 2 * KVH * HDIM), D ** -0.5, 0.125, ((0, 8),)),
        "w_out": centred(seeds[3], (H * HDIM, D), (max(D * 16 // SEQ_LEN, 1)) ** -0.5, 3.0, ((0, 8),)),
        "gain_mlp": jnp.clip(1.0 + 0.1 * jax.random.normal(seeds[4], (D,), jnp.float32), 0.5, 1.5).astype(jnp.bfloat16),
        "w_gate_up": centred(seeds[5], (D, 2 * FF), D ** -0.5, 0.125, ((0, 8),)),
        "w_down": centred(seeds[6], (D, FF), FF ** -0.5, 0.078125, ((0, 8),)),
        "cotangent": heavy_noise(seeds[7], (BLOCKS, SLAB, D), 1.0, 6.0, ((0, 8), (1, 4)), (0, 2, 8, 2.0)),
    }


@jax.custom_vjp
def low(v):
    return lax.optimization_barrier(v.astype(jnp.bfloat16)).astype(jnp.float32)

@jax.custom_vjp
def low_back(v):
    return v

def low_keep(v):
    return (low(v), None)

def low_pass(kept, grad):
    return (grad,)

def back_keep(v):
    return (v, None)

def back_low(kept, grad):
    return (low(grad),)
low.defvjp(low_keep, low_pass)
low_back.defvjp(back_keep, back_low)
epsilon = 1e-05
highest = lax.Precision.HIGHEST

def rotate(vector, cosine_table, sine_table):
    half_width = vector.shape[-1] // 2
    turned = jnp.concatenate([-vector[..., half_width:], vector[..., :half_width]], axis=-1)
    return vector * cosine_table + turned * sine_table

def angle_table(offset, length, width):
    half_width = width // 2
    frequency = 1.0 / 10000.0 ** (jnp.arange(half_width, dtype=jnp.float32) * (2.0 / width))
    places = (offset + jnp.arange(length, dtype=jnp.int32)).astype(jnp.float32)
    angles = places[:, None] * frequency[None, :]
    angles = jnp.concatenate([angles, angles], axis=1)
    return (jnp.cos(angles)[:, None, :], jnp.sin(angles)[:, None, :])

def normalize(vector):
    return vector * lax.rsqrt(lax.optimization_barrier(jnp.mean(vector * vector, axis=-1, keepdims=True)) + epsilon)

def attend(queries, keys, values):
    length = queries.shape[0]
    block_rows = min(512, length)
    group_size = H // KVH
    factor = HDIM ** (-0.5)
    key_places = jnp.arange(length, dtype=jnp.int32)
    grouped = queries.reshape(length, KVH, group_size, HDIM).transpose(1, 0, 2, 3)

    def one_head(operands):
        head_queries, head_keys, head_values = operands

        def one_block(row_start):
            query_block = lax.dynamic_slice_in_dim(head_queries, row_start, block_rows, 0)
            scores = jnp.einsum('qgd,kd->gqk', query_block, head_keys, precision=highest) * factor
            scores = low_back(scores)
            query_places = row_start + jnp.arange(block_rows, dtype=jnp.int32)
            causal = key_places[None, :] <= query_places[:, None]
            scores = jnp.where(causal[None], scores, -1e+30)
            row_max = lax.optimization_barrier(jnp.max(scores, axis=-1, keepdims=True))
            expo = jnp.exp(scores - row_max)
            probs = low(expo / lax.optimization_barrier(jnp.sum(expo, axis=-1, keepdims=True)))
            return jnp.einsum('gqk,kd->qgd', probs, head_values, precision=highest)
        starts = jnp.arange(length // block_rows, dtype=jnp.int32) * block_rows
        blocks = lax.map(jax.checkpoint(one_block), starts)
        return blocks.reshape(length, group_size, HDIM)
    heads = lax.map(one_head, (grouped, keys.transpose(1, 0, 2), values.transpose(1, 0, 2)))
    return heads.transpose(1, 0, 2, 3).reshape(length, H, HDIM)

def layer(inputs, gain_attn, w_qkv, w_out, gain_mlp, w_gate_up, w_down):
    length = inputs.shape[0]
    width_q = H * HDIM
    width_kv = KVH * HDIM
    cosine_table, sine_table = angle_table(0, length, HDIM)
    normed = low(normalize(inputs) * gain_attn)
    projected = low_back(jnp.dot(normed, w_qkv, precision=highest))
    queries = rotate(projected[:, :width_q].reshape(length, H, HDIM), cosine_table, sine_table)
    keys = rotate(projected[:, width_q:width_q + width_kv].reshape(length, KVH, HDIM), cosine_table, sine_table)
    values = projected[:, width_q + width_kv:].reshape(length, KVH, HDIM)
    queries = low_back(low(queries))
    keys = low_back(low(keys))
    values = low_back(low(values))
    mixed = low_back(low(attend(queries, keys, values).reshape(length, width_q)))
    branch = low_back(jnp.dot(mixed, w_out, precision=highest))
    middle = inputs + branch
    normed_two = low(normalize(middle) * gain_mlp)
    gate_up = low_back(jnp.dot(normed_two, w_gate_up, precision=highest))
    hidden = low(jax.nn.silu(gate_up[:, :FF]) * gate_up[:, FF:])
    feed = low_back(jnp.dot(hidden, w_down.T, precision=highest))
    return middle + feed

def reference(tokens, gain_attn, w_qkv, w_out, gain_mlp, w_gate_up, w_down, cotangent):
    floats = tuple((argument.astype(jnp.float32) for argument in (tokens, gain_attn, w_qkv, w_out, gain_mlp, w_gate_up, w_down)))
    floats = (floats[0].reshape(SEQS, SEQ_LEN, D),) + floats[1:]

    def forward(sequences, gain_one, weight_qkv, weight_out, gain_two, weight_gate_up, weight_down):

        def seq_step(carried, sequence):
            return (carried, layer(sequence, gain_one, weight_qkv, weight_out, gain_two, weight_gate_up, weight_down))
        _, layer_out = lax.scan(seq_step, jnp.zeros((), jnp.float32), sequences)
        return layer_out
    layer_out, pullback = jax.vjp(forward, *floats)
    grads = pullback(cotangent.astype(jnp.float32).reshape(SEQS, SEQ_LEN, D))
    return (layer_out.reshape(tokens.shape).astype(jnp.bfloat16), grads[0].reshape(tokens.shape), grads[2], grads[3], grads[5], grads[6], grads[1], grads[4])
```

```python
import functools

import jax
import jax.numpy as jnp
from jax import lax
from jax.experimental import pallas as pl
from jax.experimental.pallas import tpu as pltpu
from jax.sharding import PartitionSpec as P

H = 32
KVH = 4
HDIM = 64
FF = 5632
SEQ_LEN = 8192
GROUP = H // KVH

epsilon = 1e-05
low = jnp.bfloat16
wide = jnp.float32


def dot(left, right, left_dim, right_dim):
    return lax.dot_general(
        left, right, (((left_dim,), (right_dim,)), ((), ())), preferred_element_type=wide
    )


def head_columns(ref, chunk, per_chunk):
    return jnp.concatenate(
        [ref[h * HDIM : (h + 1) * HDIM, :] for h in range(chunk * per_chunk, (chunk + 1) * per_chunk)],
        axis=1,
    )


def causal(offset, first, key_block, tile, copies):
    key_places = offset + lax.broadcasted_iota(jnp.int32, (key_block, tile), 0)
    query_places = first + lax.broadcasted_iota(jnp.int32, (key_block, tile), 1)
    return jnp.concatenate([key_places <= query_places] * copies, axis=1)


def attend_kernel(places, q_ref, k_ref, v_ref, mixed_ref, lse_ref, max_s, sum_s, *, key_block, per_chunk):
    tile = q_ref.shape[1]
    chunks = GROUP // per_chunk
    first = places[pl.program_id(0)]
    queries = [head_columns(q_ref, c, per_chunk) for c in range(chunks)]
    max_s[...] = jnp.full(max_s.shape, -1e30, wide)
    sum_s[...] = jnp.zeros(sum_s.shape, wide)

    def step(index, masked):
        offset = pl.multiple_of(index * key_block, key_block)
        keys = k_ref[pl.ds(offset, key_block), :]
        values = v_ref[:, pl.ds(offset, key_block)]
        if masked:
            keep = causal(offset, first, key_block, tile, per_chunk)
        for c in range(chunks):
            scores = jnp.dot(keys, queries[c], preferred_element_type=wide)
            if masked:
                scores = jnp.where(keep, scores, -1e30)
            old = max_s[c]
            new = jnp.maximum(old, jnp.max(scores, axis=0, keepdims=True))
            probs = jnp.exp(scores - new).astype(low)
            max_s[c] = new
            sum_s[c] = sum_s[c] * jnp.exp(old - new) + jnp.dot(
                values, probs, preferred_element_type=wide
            )

    full = first // key_block
    lax.fori_loop(0, full, lambda i, _: (step(i, False), 0)[1], 0)
    step(full, True)
    for c in range(chunks):
        sums = sum_s[c]
        total = sums[HDIM : HDIM + 1, :]
        mixed = sums[:HDIM, :] * (1.0 / total)
        lse = max_s[c] + jnp.log(total)
        for i in range(per_chunk):
            h = c * per_chunk + i
            mixed_ref[h * HDIM : (h + 1) * HDIM, :] = mixed[:, i * tile : (i + 1) * tile]
            lse_ref[0, h : h + 1, :] = lse[:, i * tile : (i + 1) * tile]


def attend(places, queries, keys, values_ones, tile, key_block=512, per_chunk=4):
    features, tokens = queries.shape
    tiles = tokens // tile
    chunks = GROUP // per_chunk
    pairs = GROUP * tokens * keys.shape[0] // 2
    return pl.pallas_call(
        functools.partial(attend_kernel, key_block=key_block, per_chunk=per_chunk),
        grid_spec=pltpu.PrefetchScalarGridSpec(
            num_scalar_prefetch=1,
            grid=(tiles,),
            in_specs=[
                pl.BlockSpec((features, tile), lambda i, p: (0, i)),
                pl.BlockSpec(keys.shape, lambda i, p: (0, 0)),
                pl.BlockSpec(values_ones.shape, lambda i, p: (0, 0)),
            ],
            out_specs=[
                pl.BlockSpec((features, tile), lambda i, p: (0, i)),
                pl.BlockSpec((1, GROUP, tile), lambda i, p: (i, 0, 0)),
            ],
            scratch_shapes=[
                pltpu.VMEM((chunks, 1, per_chunk * tile), wide),
                pltpu.VMEM((chunks, values_ones.shape[0], per_chunk * tile), wide),
            ],
        ),
        out_shape=[
            jax.ShapeDtypeStruct((features, tokens), wide),
            jax.ShapeDtypeStruct((tiles, GROUP, tile), wide),
        ],
        compiler_params=pltpu.CompilerParams(vmem_limit_bytes=40 << 20),
        cost_estimate=pl.CostEstimate(
            flops=pairs * HDIM * 16, bytes_accessed=16 << 20, transcendentals=pairs
        ),
        name="attend",
    )(places, queries, keys, values_ones)


def attend_back_kernel(
    places, qt_ref, q_ref, gt_ref, g_ref, mixed_ref, lse_ref, k_ref, v_ref, kt_ref, gq_ref, gk_ref, gv_ref, gq_s,
    *, key_block, per_chunk,
):
    tile = qt_ref.shape[1]
    chunks = GROUP // per_chunk
    columns = per_chunk * tile
    first = places[pl.program_id(0)]

    @pl.when(pl.program_id(0) == 0)
    def _():
        gk_ref[...] = jnp.zeros(gk_ref.shape, wide)
        gv_ref[...] = jnp.zeros(gv_ref.shape, wide)

    queries = [head_columns(qt_ref, c, per_chunk) for c in range(chunks)]
    grads = [head_columns(gt_ref, c, per_chunk) for c in range(chunks)]
    inner = [
        jnp.sum(grads[c].astype(wide) * head_columns(mixed_ref, c, per_chunk), axis=0, keepdims=True)
        for c in range(chunks)
    ]
    lse = [
        jnp.concatenate([lse_ref[0, c * per_chunk + i : c * per_chunk + i + 1, :] for i in range(per_chunk)], axis=1)
        for c in range(chunks)
    ]
    gq_s[...] = jnp.zeros(gq_s.shape, wide)

    def step(index, masked):
        offset = pl.multiple_of(index * key_block, key_block)
        keys = k_ref[pl.ds(offset, key_block), :]
        values = v_ref[pl.ds(offset, key_block), :]
        keys_t = kt_ref[:, pl.ds(offset, key_block)]
        if masked:
            keep = causal(offset, first, key_block, tile, per_chunk)
        grad_k = grad_v = None
        for c in range(chunks):
            scores = jnp.dot(keys, queries[c], preferred_element_type=wide)
            if masked:
                scores = jnp.where(keep, scores, -1e30)
            probs = jnp.exp(scores - lse[c])
            grad_probs = jnp.dot(values, grads[c], preferred_element_type=wide)
            grad_scores = (probs * (grad_probs - inner[c])).astype(low)
            rows = slice(c * columns, (c + 1) * columns)
            more_k = jnp.dot(grad_scores, q_ref[0, rows, :], preferred_element_type=wide)
            more_v = jnp.dot(probs.astype(low), g_ref[0, rows, :], preferred_element_type=wide)
            gq_s[c] += jnp.dot(keys_t, grad_scores, preferred_element_type=wide)
            grad_k = more_k if grad_k is None else grad_k + more_k
            grad_v = more_v if grad_v is None else grad_v + more_v
        gk_ref[pl.ds(offset, key_block), :] += grad_k
        gv_ref[pl.ds(offset, key_block), :] += grad_v

    full = first // key_block
    lax.fori_loop(0, full, lambda i, _: (step(i, False), 0)[1], 0)
    step(full, True)
    for c in range(chunks):
        grad_q = gq_s[c] * HDIM**-0.5
        for i in range(per_chunk):
            h = c * per_chunk + i
            gq_ref[h * HDIM : (h + 1) * HDIM, :] = grad_q[:, i * tile : (i + 1) * tile]


def attend_back(places, queries_t, queries, grads_t, grads, mixed, lse, keys, values, keys_t, tile, key_block=512, per_chunk=2):
    features, tokens = queries_t.shape
    tiles = tokens // tile
    chunks = GROUP // per_chunk
    pairs = GROUP * tokens * keys.shape[0] // 2
    by_tile = pl.BlockSpec((features, tile), lambda i, p: (0, i))
    rows = pl.BlockSpec((1, GROUP * tile, HDIM), lambda i, p: (i, 0, 0))

    def whole(value):
        return pl.BlockSpec(value.shape, lambda i, p: (0, 0))

    return pl.pallas_call(
        functools.partial(attend_back_kernel, key_block=key_block, per_chunk=per_chunk),
        grid_spec=pltpu.PrefetchScalarGridSpec(
            num_scalar_prefetch=1,
            grid=(tiles,),
            in_specs=[
                by_tile,
                rows,
                by_tile,
                rows,
                by_tile,
                pl.BlockSpec((1, GROUP, tile), lambda i, p: (i, 0, 0)),
                whole(keys),
                whole(values),
                whole(keys_t),
            ],
            out_specs=[by_tile, whole(keys), whole(values)],
            scratch_shapes=[pltpu.VMEM((chunks, HDIM, per_chunk * tile), wide)],
        ),
        out_shape=[
            jax.ShapeDtypeStruct((features, tokens), wide),
            jax.ShapeDtypeStruct(keys.shape, wide),
            jax.ShapeDtypeStruct(values.shape, wide),
        ],
        compiler_params=pltpu.CompilerParams(vmem_limit_bytes=48 << 20),
        cost_estimate=pl.CostEstimate(
            flops=pairs * HDIM * 40, bytes_accessed=24 << 20, transcendentals=pairs
        ),
        name="attend_back",
    )(places, queries_t, queries, grads_t, grads, mixed, lse, keys, values, keys_t)


def from_core(value):
    return lax.ppermute(value, "seq", [(i, i ^ 1) for i in range(lax.axis_size("seq"))])


def from_chip(value):
    return lax.ppermute(value, "seq", [(i, i ^ 2) for i in range(lax.axis_size("seq"))])


def seq_gather(value):
    pair = jnp.stack([value, from_chip(value)])
    other = from_core(pair)
    return jnp.stack([pair[0], other[0], pair[1], other[1]])


def seq_sum(parts):
    sent = jnp.stack([parts[1], parts[3]]).astype(low)
    came = from_core(sent).astype(wide)
    far = (parts[2] + came[1]).astype(low)
    return parts[0] + came[0] + from_chip(far).astype(wide)


def slots_by_index(value, axis):
    own = lax.axis_index("seq")
    shape = value.shape
    split = value.reshape(shape[:axis] + (2, 2) + shape[axis + 1 :])
    split = jnp.where(own % 2 == 1, jnp.flip(split, axis + 1), split)
    split = jnp.where(own // 2 == 1, jnp.flip(split, axis), split)
    return split.reshape(shape)


def turn(vectors, cosine, sine):
    half = HDIM // 2
    first, second = vectors[:, :half], vectors[:, half:]
    return jnp.concatenate([first * cosine - second * sine, second * cosine + first * sine], axis=1)


def norm_back(grad_hat, normal, inverse):
    return inverse * (grad_hat - normal * jnp.mean(grad_hat * normal, axis=-1, keepdims=True))


def inverse_rms(values):
    return lax.rsqrt(jnp.mean(values * values, axis=-1, keepdims=True) + epsilon)


def local(tokens, gain_attn, w_qkv, w_out, gain_mlp, w_gate_up, w_down, cotangent):
    width = tokens.shape[-1]
    seq_parts = lax.axis_size("seq")
    blocks = lax.axis_size("fsdp")
    assert seq_parts == KVH == 4
    own_tokens = tokens.reshape(-1, width)
    rows = own_tokens.shape[0]
    tile = rows // 2
    slab = rows * seq_parts
    span = SEQ_LEN // slab
    seq_index = lax.axis_index("seq")
    position = lax.axis_index("fsdp") % span
    mirrored = span - 1 - position
    sequences = [list(range(i, i + span)) for i in range(0, blocks, span)]
    groups = None if span == blocks else sequences
    width_q = H * HDIM
    width_kv = KVH * HDIM
    q_part = GROUP * HDIM
    ff_part = FF // seq_parts

    def mirror(half):
        pairs = [(g[i], g[span - 1 - i]) for g in sequences for i in range(span)]
        return lax.ppermute(half, "fsdp", pairs)

    def balance(value):
        return jnp.concatenate([value[:tile], mirror(value[tile:])], axis=0)

    def part(weight, start, size):
        return lax.dynamic_slice_in_dim(weight, start + seq_index * size, size, 1)

    def fsdp_gather(value):
        return lax.all_gather(value, "fsdp", axis=0, tiled=True)

    def fsdp_sum(value):
        return lax.psum_scatter(value.astype(low), "fsdp", scatter_dimension=0, tiled=True)

    def by_rows(value):
        return value.reshape(slab, -1)

    def slots(value):
        return value.reshape(seq_parts, rows, -1)

    inputs_low = balance(own_tokens)
    grad_feed_low = balance(cotangent.reshape(-1, width))
    gains = fsdp_gather(jnp.stack([gain_attn, gain_mlp], axis=1))
    qkv_part = fsdp_gather(
        jnp.concatenate(
            [
                part(w_qkv, 0, q_part),
                part(w_qkv, width_q, HDIM),
                part(w_qkv, width_q + width_kv, HDIM),
            ],
            axis=1,
        )
    )
    out_columns = fsdp_gather(part(w_out, 0, width // seq_parts))
    out_part = lax.all_to_all(out_columns, "seq", split_axis=0, concat_axis=1, tiled=True)
    gate_up_part = fsdp_gather(
        jnp.concatenate([part(w_gate_up, 0, ff_part), part(w_gate_up, FF, ff_part)], axis=1)
    )
    down_part = fsdp_gather(part(w_down, 0, ff_part))
    gain_one = gains[:, 0].astype(wide)
    gain_two = gains[:, 1].astype(wide)

    all_inputs = by_rows(seq_gather(inputs_low)).astype(wide)
    normed_one = (all_inputs * inverse_rms(all_inputs) * gain_one).astype(low)
    projected = dot(qkv_part, normed_one, 0, 1)
    frequency = 1.0 / 10000.0 ** (jnp.arange(HDIM // 2, dtype=wide) * (2.0 / HDIM))
    row = jnp.arange(slab, dtype=jnp.int32)
    within = (row // rows ^ seq_index) * rows + row % rows
    row_places = jnp.where(row % rows < tile, position, mirrored) * slab + within
    angles = frequency[:, None] * row_places.astype(wide)[None, :]
    cosine, sine = jnp.cos(angles), jnp.sin(angles)
    places = row_places[::tile]
    queries = turn(projected[:q_part].reshape(GROUP, HDIM, slab), cosine, sine) * HDIM**-0.5
    queries = queries.reshape(q_part, slab).astype(low)
    keys_own = turn(projected[q_part : q_part + HDIM].reshape(1, HDIM, slab), cosine, sine)[0]
    kv_own = jnp.concatenate([keys_own, projected[q_part + HDIM :]], axis=0).astype(low)
    kv_own = slots_by_index(kv_own.reshape(2 * HDIM, seq_parts, 2, tile), 1)
    kv_all = lax.all_gather(kv_own, "fsdp", axis_index_groups=groups)
    kv_all = jnp.stack([kv_all[:, :, :, 0], kv_all[::-1, :, :, 1]], axis=3)
    kv_all = kv_all.transpose(1, 0, 2, 3, 4).reshape(2 * HDIM, SEQ_LEN)
    keys_t, values_t = kv_all[:HDIM], kv_all[HDIM:]
    keys, values = keys_t.T, values_t.T
    values_ones = jnp.concatenate([values_t, jnp.ones((8, SEQ_LEN), low)], axis=0)
    mixed_wide, lse = attend(places, queries, keys, values_ones, tile)
    mixed = mixed_wide.astype(low)

    inputs = inputs_low.astype(wide)
    middle = inputs + seq_sum(slots(dot(mixed, out_part, 0, 0)))
    inverse_two = inverse_rms(middle)
    hat_two = middle * inverse_two
    normed_two = by_rows(seq_gather((hat_two * gain_two).astype(low)))

    gate_up = jnp.dot(normed_two, gate_up_part, preferred_element_type=wide)
    gate, up = gate_up[:, :ff_part], gate_up[:, ff_part:]
    sigmoid = jax.nn.sigmoid(gate)
    silu = gate * sigmoid
    hidden = (silu * up).astype(low)
    feed = seq_sum(slots(dot(hidden, down_part, 1, 1)))
    layer_out = balance((middle + feed).astype(low))

    grad_feed = by_rows(seq_gather(grad_feed_low))
    grad_hidden = jnp.dot(grad_feed, down_part, preferred_element_type=wide)
    grad_gate = grad_hidden * up * sigmoid * (1.0 + gate * (1.0 - sigmoid))
    grad_pre = jnp.concatenate([grad_gate, grad_hidden * silu], axis=1).astype(low)
    grad_down = fsdp_sum(dot(grad_feed, hidden, 0, 0))
    grad_gate_up = fsdp_sum(dot(normed_two, grad_pre, 0, 0))
    grad_normed_two = seq_sum(slots(dot(grad_pre, gate_up_part, 1, 1)))
    grad_middle = grad_feed_low.astype(wide) + norm_back(
        grad_normed_two * gain_two, hat_two, inverse_two
    )
    grad_branch = by_rows(seq_gather(grad_middle.astype(low)))
    grad_out_rows = dot(mixed, grad_branch, 1, 0).astype(low)
    grad_out = fsdp_sum(lax.all_to_all(grad_out_rows, "seq", split_axis=1, concat_axis=0, tiled=True))

    grad_mixed = dot(out_part, grad_branch, 1, 1).astype(low)

    def head_rows(value):
        by_head = value.reshape(GROUP, HDIM, slab // tile, tile).transpose(2, 0, 3, 1)
        return by_head.reshape(slab // tile, GROUP * tile, HDIM)

    grad_q, grad_k, grad_v = attend_back(
        places, queries, head_rows(queries), grad_mixed, head_rows(grad_mixed),
        mixed_wide, lse, keys, values, keys_t, tile,
    )
    grad_kv = jnp.concatenate([grad_k, grad_v], axis=1).astype(low)
    grad_kv = grad_kv.reshape(span, seq_parts, 2, tile, 2 * HDIM)
    grad_kv = jnp.stack([grad_kv[:, :, 0], grad_kv[::-1, :, 1]], axis=2)
    grad_kv = lax.psum_scatter(grad_kv, "fsdp", scatter_dimension=0, axis_index_groups=groups)
    grad_kv = slots_by_index(grad_kv, 0).reshape(slab, 2 * HDIM).T.astype(wide)
    grad_q = grad_q.astype(low).astype(wide)
    grad_projected = jnp.concatenate(
        [
            turn(grad_q.reshape(GROUP, HDIM, slab), cosine, -sine).reshape(q_part, slab),
            turn(grad_kv[:HDIM].reshape(1, HDIM, slab), cosine, -sine)[0],
            grad_kv[HDIM:],
        ],
        axis=0,
    ).astype(low)
    grad_normed_one = seq_sum(slots(dot(grad_projected, qkv_part, 0, 1)))
    grad_qkv = fsdp_sum(dot(normed_one, grad_projected, 0, 1))
    inverse_one = inverse_rms(inputs)
    grad_inputs = grad_middle + norm_back(
        grad_normed_one * gain_one, inputs * inverse_one, inverse_one
    )
    grad_inputs = balance(grad_inputs)

    def columns_of(value):
        return lax.all_gather(value, "seq").astype(wide)

    def side_by_side(value, start, size):
        return value[:, :, start : start + size].transpose(1, 0, 2).reshape(value.shape[1], -1)

    down = columns_of(grad_down)
    gate_up_all = columns_of(grad_gate_up)
    out_all = columns_of(grad_out)
    qkv_all = columns_of(grad_qkv)
    weight_grad_down = side_by_side(down, 0, ff_part)
    weight_grad_gate_up = jnp.concatenate(
        [side_by_side(gate_up_all, 0, ff_part), side_by_side(gate_up_all, ff_part, ff_part)], axis=1
    )
    weight_grad_out = side_by_side(out_all, 0, width // seq_parts)
    weight_grad_qkv = jnp.concatenate(
        [
            side_by_side(qkv_all, 0, q_part),
            side_by_side(qkv_all, q_part, HDIM),
            side_by_side(qkv_all, q_part + HDIM, HDIM),
        ],
        axis=1,
    )
    grad_gain_one = jnp.sum(w_qkv.astype(wide) * weight_grad_qkv, axis=1) / gain_attn.astype(wide)
    grad_gain_two = jnp.sum(w_gate_up.astype(wide) * weight_grad_gate_up, axis=1) / gain_mlp.astype(wide)
    return (
        layer_out.reshape(tokens.shape),
        grad_inputs.reshape(tokens.shape),
        weight_grad_qkv,
        weight_grad_out,
        weight_grad_gate_up,
        weight_grad_down,
        grad_gain_one,
        grad_gain_two,
    )


def solution(mesh):
    by_token = P("fsdp", "seq", None)
    by_row = P("fsdp", None)
    return jax.shard_map(
        local,
        mesh=mesh,
        in_specs=(by_token, P("fsdp"), by_row, by_row, P("fsdp"), by_row, by_row, by_token),
        out_specs=(by_token, by_token, by_row, by_row, by_row, by_row, P("fsdp"), P("fsdp")),
        check_vma=False,
    )
```

```python
import functools

import jax
import jax.numpy as jnp
from jax import lax
from jax.experimental import pallas as pl
from jax.experimental.pallas import tpu as pltpu
from jax.sharding import PartitionSpec as P

H = 32
KVH = 4
HDIM = 64
FF = 5632
SEQ_LEN = 8192
GROUP = H // KVH

epsilon = 1e-05
low = jnp.bfloat16
wide = jnp.float32


def dot(left, right, left_dim, right_dim):
    return lax.dot_general(
        left, right, (((left_dim,), (right_dim,)), ((), ())), preferred_element_type=wide
    )


def head_columns(ref, chunk, per_chunk):
    return jnp.concatenate(
        [ref[h * HDIM : (h + 1) * HDIM, :] for h in range(chunk * per_chunk, (chunk + 1) * per_chunk)],
        axis=1,
    )


def causal(offset, first, key_block, tile, copies):
    key_places = offset + lax.broadcasted_iota(jnp.int32, (key_block, tile), 0)
    query_places = first + lax.broadcasted_iota(jnp.int32, (key_block, tile), 1)
    return jnp.concatenate([key_places <= query_places] * copies, axis=1)


def each_piece(places, span, tiles, tile, visit):
    own = places[tiles]

    def one(n, _):
        block, rest = n // tiles, n % tiles
        index, half = rest // 2, rest % 2
        sender = jnp.where(half == 0, block, span - 1 - block)
        visit(
            sender,
            pl.multiple_of(((index ^ own) * 2 + half) * tile, tile),
            pl.multiple_of(n * tile, tile),
        )
        return 0

    lax.fori_loop(0, span * tiles, one, 0, unroll=8)


def unpack_kernel(places, kv_ref, keys_ref, values_ref, kt_ref, ones_ref, *, tile, tiles):
    ones_ref[HDIM:, :] = jnp.ones((8, ones_ref.shape[1]), low)

    def visit(sender, start, place):
        piece = kv_ref[sender, :, pl.ds(start, tile)]
        kt_ref[:, pl.ds(place, tile)] = piece[:HDIM]
        ones_ref[:HDIM, pl.ds(place, tile)] = piece[HDIM:]
        turned = piece.astype(wide).T.astype(low)
        keys_ref[pl.ds(place, tile), :] = turned[:, :HDIM]
        values_ref[pl.ds(place, tile), :] = turned[:, HDIM:]

    each_piece(places, kv_ref.shape[0], tiles, tile, visit)


def whole_block(shape):
    return pl.BlockSpec(shape, lambda i, p: (0,) * len(shape))


def unpack(places, kv, tile):
    span, _, slab = kv.shape
    length = span * slab
    shapes = [(length, HDIM), (length, HDIM), (HDIM, length), (HDIM + 8, length)]
    return pl.pallas_call(
        functools.partial(unpack_kernel, tile=tile, tiles=slab // tile),
        grid_spec=pltpu.PrefetchScalarGridSpec(
            num_scalar_prefetch=1,
            grid=(1,),
            in_specs=[whole_block(kv.shape)],
            out_specs=[whole_block(shape) for shape in shapes],
        ),
        out_shape=[jax.ShapeDtypeStruct(shape, low) for shape in shapes],
        compiler_params=pltpu.CompilerParams(vmem_limit_bytes=32 << 20),
        name="unpack",
    )(places, kv)


def attend_kernel(places, q_ref, keys_ref, values_ref, mixed_ref, lse_ref, max_s, sum_s, *, key_block, per_chunk, base):
    tile = q_ref.shape[1]
    chunks = GROUP // per_chunk
    first = places[pl.program_id(0) + base]
    queries = [head_columns(q_ref, c, per_chunk) for c in range(chunks)]
    max_s[...] = jnp.full(max_s.shape, -1e30, wide)
    sum_s[...] = jnp.zeros(sum_s.shape, wide)

    def step(index, masked):
        offset = pl.multiple_of(index * key_block, key_block)
        keys = keys_ref[pl.ds(offset, key_block), :]
        values = values_ref[:, pl.ds(offset, key_block)]
        if masked:
            keep = causal(offset, first, key_block, tile, per_chunk)
        for c in range(chunks):
            scores = jnp.dot(keys, queries[c], preferred_element_type=wide)
            if masked:
                scores = jnp.where(keep, scores, -1e30)
            old = max_s[c]
            new = jnp.maximum(old, jnp.max(scores, axis=0, keepdims=True))
            probs = jnp.exp(scores - new).astype(low)
            max_s[c] = new
            sum_s[c] = sum_s[c] * jnp.exp(old - new) + jnp.dot(
                values, probs, preferred_element_type=wide
            )

    full = first // key_block
    lax.fori_loop(0, full, lambda i, _: (step(i, False), 0)[1], 0)
    step(full, True)
    for c in range(chunks):
        sums = sum_s[c]
        total = sums[HDIM : HDIM + 1, :]
        mixed = sums[:HDIM, :] * (1.0 / total)
        lse = max_s[c] + jnp.log(total)
        for i in range(per_chunk):
            h = c * per_chunk + i
            mixed_ref[h * HDIM : (h + 1) * HDIM, :] = mixed[:, i * tile : (i + 1) * tile]
            lse_ref[0, h : h + 1, :] = lse[:, i * tile : (i + 1) * tile]


def attend(places, queries, keys, values_ones, tile, base, tiles, key_block=512, per_chunk=8):
    features, _ = queries.shape
    length = keys.shape[0]
    chunks = GROUP // per_chunk
    pairs = GROUP * tiles * tile * length // 2
    return pl.pallas_call(
        functools.partial(attend_kernel, key_block=key_block, per_chunk=per_chunk, base=base),
        grid_spec=pltpu.PrefetchScalarGridSpec(
            num_scalar_prefetch=1,
            grid=(tiles,),
            in_specs=[
                pl.BlockSpec((features, tile), lambda i, p: (0, i + base)),
                whole_block(keys.shape),
                whole_block(values_ones.shape),
            ],
            out_specs=[
                pl.BlockSpec((features, tile), lambda i, p: (0, i)),
                pl.BlockSpec((1, GROUP, tile), lambda i, p: (i, 0, 0)),
            ],
            scratch_shapes=[
                pltpu.VMEM((chunks, 1, per_chunk * tile), wide),
                pltpu.VMEM((chunks, HDIM + 8, per_chunk * tile), wide),
            ],
        ),
        out_shape=[
            jax.ShapeDtypeStruct((features, tiles * tile), wide),
            jax.ShapeDtypeStruct((tiles, GROUP, tile), wide),
        ],
        compiler_params=pltpu.CompilerParams(vmem_limit_bytes=40 << 20),
        cost_estimate=pl.CostEstimate(
            flops=pairs * HDIM * 16, bytes_accessed=8 << 20, transcendentals=pairs
        ),
        name="attend",
    )(places, queries, keys, values_ones)


def attend_back_kernel(places, *refs, key_block, per_chunk, base, tiles, slab, last):
    q_ref, g_ref, mixed_ref, lse_ref, keys_ref, values_ref, kt_ref = refs[:7]
    if last:
        k_before, v_before, gq_ref, gkv_ref, gq_s, gk_s, gv_s = refs[7:]
    else:
        gq_ref, gk_s, gv_s, gq_s = refs[7:]
    tile = q_ref.shape[1]
    chunks = GROUP // per_chunk
    first = places[pl.program_id(0) + base]

    @pl.when(pl.program_id(0) == 0)
    def _():
        gk_s[...] = k_before[...] if last else jnp.zeros(gk_s.shape, wide)
        gv_s[...] = v_before[...] if last else jnp.zeros(gv_s.shape, wide)

    queries = [head_columns(q_ref, c, per_chunk) for c in range(chunks)]
    grads = [head_columns(g_ref, c, per_chunk) for c in range(chunks)]
    inner = [
        jnp.sum(grads[c].astype(wide) * head_columns(mixed_ref, c, per_chunk), axis=0, keepdims=True)
        for c in range(chunks)
    ]
    lse = [
        jnp.concatenate([lse_ref[0, c * per_chunk + i : c * per_chunk + i + 1, :] for i in range(per_chunk)], axis=1)
        for c in range(chunks)
    ]
    gq_s[...] = jnp.zeros(gq_s.shape, wide)

    def step(index, masked):
        offset = pl.multiple_of(index * key_block, key_block)
        keys = keys_ref[pl.ds(offset, key_block), :]
        values = values_ref[pl.ds(offset, key_block), :]
        keys_t = kt_ref[:, pl.ds(offset, key_block)]
        if masked:
            keep = causal(offset, first, key_block, tile, per_chunk)
        grad_k = grad_v = None
        for c in range(chunks):
            scores = jnp.dot(keys, queries[c], preferred_element_type=wide)
            if masked:
                scores = jnp.where(keep, scores, -1e30)
            probs = jnp.exp(scores - lse[c])
            grad_probs = jnp.dot(values, grads[c], preferred_element_type=wide)
            grad_scores = (probs * (grad_probs - inner[c])).astype(low)
            more_k = dot(grad_scores, queries[c], 1, 1)
            more_v = dot(probs.astype(low), grads[c], 1, 1)
            gq_s[c] += jnp.dot(keys_t, grad_scores, preferred_element_type=wide)
            grad_k = more_k if grad_k is None else grad_k + more_k
            grad_v = more_v if grad_v is None else grad_v + more_v
        gk_s[pl.ds(offset, key_block), :] += grad_k
        gv_s[pl.ds(offset, key_block), :] += grad_v

    full = first // key_block
    lax.fori_loop(0, full, lambda i, _: (step(i, False), 0)[1], 0)
    step(full, True)
    for c in range(chunks):
        grad_q = gq_s[c] * HDIM**-0.5
        for i in range(per_chunk):
            h = c * per_chunk + i
            gq_ref[h * HDIM : (h + 1) * HDIM, :] = grad_q[:, i * tile : (i + 1) * tile]

    if last:

        @pl.when(pl.program_id(0) == tiles - 1)
        def _():
            def visit(sender, start, place):
                both = jnp.concatenate([gk_s[pl.ds(place, tile), :], gv_s[pl.ds(place, tile), :]], axis=1)
                gkv_ref[sender, :, pl.ds(start, tile)] = both.T.astype(low)

            each_piece(places, gkv_ref.shape[0], slab // tile, tile, visit)


def attend_back(
    places, queries, grads, mixed, lse, keys, values, keys_t, tile, base, tiles, slab, before=None,
    key_block=512, per_chunk=8,
):
    features, _ = queries.shape
    length = keys.shape[0]
    span = length // slab
    chunks = GROUP // per_chunk
    pairs = GROUP * tiles * tile * length // 2
    last = before is not None
    by_tile = pl.BlockSpec((features, tile), lambda i, p: (0, i))
    packed = (span, 2 * HDIM, slab)
    sums = [pltpu.VMEM((length, HDIM), wide)] * 2
    return pl.pallas_call(
        functools.partial(
            attend_back_kernel,
            key_block=key_block, per_chunk=per_chunk, base=base, tiles=tiles, slab=slab, last=last,
        ),
        grid_spec=pltpu.PrefetchScalarGridSpec(
            num_scalar_prefetch=1,
            grid=(tiles,),
            in_specs=[
                pl.BlockSpec((features, tile), lambda i, p: (0, i + base)),
                by_tile,
                by_tile,
                pl.BlockSpec((1, GROUP, tile), lambda i, p: (i, 0, 0)),
                whole_block(keys.shape),
                whole_block(values.shape),
                whole_block(keys_t.shape),
            ]
            + [whole_block(keys.shape)] * (2 * last),
            out_specs=[by_tile] + ([whole_block(packed)] if last else [whole_block(keys.shape)] * 2),
            scratch_shapes=[pltpu.VMEM((chunks, HDIM, per_chunk * tile), wide)] + sums * last,
        ),
        out_shape=[jax.ShapeDtypeStruct((features, tiles * tile), wide)]
        + ([jax.ShapeDtypeStruct(packed, low)] if last else [jax.ShapeDtypeStruct(keys.shape, wide)] * 2),
        compiler_params=pltpu.CompilerParams(vmem_limit_bytes=56 << 20),
        cost_estimate=pl.CostEstimate(
            flops=pairs * HDIM * 40, bytes_accessed=16 << 20, transcendentals=pairs
        ),
        name="attend_back",
    )(places, queries, grads, mixed, lse, keys, values, keys_t, *(before or ()))


def widen_kernel(own, *refs):
    out_ref = refs[-1]
    for i, ref in enumerate(refs[:-1]):

        @pl.when(pl.program_id(0) == i)
        def _(ref=ref):
            out_ref[...] = ref[...].astype(wide)


def widen(own, pieces, at=0, columns=None):
    parts = len(pieces)
    rows = pieces[0].shape[0]
    columns = columns or pieces[0].shape[1]
    return pl.pallas_call(
        widen_kernel,
        grid_spec=pltpu.PrefetchScalarGridSpec(
            num_scalar_prefetch=1,
            grid=(parts,),
            in_specs=[pl.BlockSpec((rows, columns), lambda i, own: (0, at))] * parts,
            out_specs=pl.BlockSpec((rows, columns), lambda i, own: (0, i ^ own[0])),
        ),
        out_shape=jax.ShapeDtypeStruct((rows, parts * columns), wide),
        compiler_params=pltpu.CompilerParams(vmem_limit_bytes=24 << 20),
        name="widen",
    )(own, *pieces)


def widen_pair_kernel(own, *refs):
    weight_ref, out_ref, total_ref = refs[-3:]
    step = pl.program_id(0)
    for i, ref in enumerate(refs[:-3]):

        @pl.when(step == i)
        def _(ref=ref):
            value = ref[...].astype(wide)
            out_ref[...] = value
            more = jnp.sum(value * weight_ref[...].astype(wide), axis=1, keepdims=True)
            total_ref[...] = jnp.where(step == 0, more, total_ref[...] + more)


def widen_pair(own, left, right, weight):
    parts = len(left)
    rows, columns = left[0].shape

    def place(i, own):
        return (0, i // parts * parts + (i % parts ^ own[0]))

    return pl.pallas_call(
        widen_pair_kernel,
        grid_spec=pltpu.PrefetchScalarGridSpec(
            num_scalar_prefetch=1,
            grid=(2 * parts,),
            in_specs=[pl.BlockSpec((rows, columns), lambda i, own: (0, 0))] * (2 * parts)
            + [pl.BlockSpec((rows, columns), place)],
            out_specs=[
                pl.BlockSpec((rows, columns), place),
                pl.BlockSpec((rows, 1), lambda i, own: (0, 0)),
            ],
        ),
        out_shape=[
            jax.ShapeDtypeStruct((rows, 2 * parts * columns), wide),
            jax.ShapeDtypeStruct((rows, 1), wide),
        ],
        compiler_params=pltpu.CompilerParams(vmem_limit_bytes=32 << 20),
        name="widen_pair",
    )(own, *left, *right, weight)


def widen_qkv_kernel(own, *refs, parts):
    weight_ref, out_ref, total_ref = refs[-3:]
    step = pl.program_id(0)

    def write(value):
        out_ref[...] = value
        more = jnp.sum(value * weight_ref[...].astype(wide), axis=1, keepdims=True)
        total_ref[...] = jnp.where(step == 0, more, total_ref[...] + more)

    for i, ref in enumerate(refs[:parts]):

        @pl.when(step == i)
        def _(ref=ref):
            write(ref[...].astype(wide))

    @pl.when(step == parts)
    def _():
        pieces = [ref[...].astype(wide) for ref in refs[parts : 2 * parts]]
        ordered = []
        for i in range(parts):
            value = pieces[i]
            for j in range(1, parts):
                value = jnp.where(own[0] == j, pieces[i ^ j], value)
            ordered.append(value)
        write(jnp.concatenate([v[:, :HDIM] for v in ordered] + [v[:, HDIM:] for v in ordered], axis=1))


def widen_qkv(own, queries, rest, weight):
    parts = len(queries)
    rows, columns = queries[0].shape[0], parts * 2 * HDIM

    def place(i, own):
        return (0, jnp.where(i < parts, i ^ own[0], parts))

    return pl.pallas_call(
        functools.partial(widen_qkv_kernel, parts=parts),
        grid_spec=pltpu.PrefetchScalarGridSpec(
            num_scalar_prefetch=1,
            grid=(parts + 1,),
            in_specs=[pl.BlockSpec((rows, columns), lambda i, own: (0, 0))] * parts
            + [pl.BlockSpec((rows, 2 * HDIM), lambda i, own: (0, 0))] * parts
            + [pl.BlockSpec((rows, columns), place)],
            out_specs=[
                pl.BlockSpec((rows, columns), place),
                pl.BlockSpec((rows, 1), lambda i, own: (0, 0)),
            ],
        ),
        out_shape=[
            jax.ShapeDtypeStruct((rows, (parts + 1) * columns), wide),
            jax.ShapeDtypeStruct((rows, 1), wide),
        ],
        compiler_params=pltpu.CompilerParams(vmem_limit_bytes=24 << 20),
        name="widen_qkv",
    )(own, *queries, *rest, weight)


def from_core(value):
    return lax.ppermute(value, "seq", [(i, i ^ 1) for i in range(lax.axis_size("seq"))])


def from_chip(value):
    return lax.ppermute(value, "seq", [(i, i ^ 2) for i in range(lax.axis_size("seq"))])


def seq_gather(value):
    far = from_chip(value)
    return [value, from_core(value), far, from_core(far)]


def seq_sum_core(parts):
    far = parts[2].astype(wide) + from_core(parts[3]).astype(wide)
    near = parts[0].astype(wide) + from_core(parts[1]).astype(wide)
    return near, far.astype(low)


def seq_sum(parts):
    near, far = seq_sum_core(parts)
    return near + from_chip(far).astype(wide)


def slots_by_index(value):
    own = lax.axis_index("seq")
    return [
        lax.dynamic_index_in_dim(value, own ^ j, 0, keepdims=False) for j in range(lax.axis_size("seq"))
    ]


def from_turn(value, by):
    size = lax.axis_size("fsdp")
    return lax.ppermute(value, "fsdp", [(i, (i + 2 * by) % size) for i in range(size)])


def from_pair(value):
    return lax.ppermute(value, "fsdp", [(i, i ^ 1) for i in range(lax.axis_size("fsdp"))])


def team_gather(value):
    half = value.shape[0] // 2
    beside, far = from_pair(value), from_chip(value)
    corner = jnp.concatenate([from_chip(beside[:half]), from_pair(far[half:])], axis=0)
    return [each for held in (value, far, beside, corner) for each in (held, from_core(held))]


def team_sum_core(parts):
    return [
        parts[i].astype(wide) + from_core(parts[i + 1]).astype(wide) for i in range(0, len(parts), 2)
    ]


def team_corner_hops(corner):
    half = corner.shape[0] // 2
    return from_chip(corner[:half]), from_pair(corner[half:])


def team_corner_add(sums, top, bottom):
    near, far, beside, _ = sums
    half = near.shape[0] // 2
    beside = jnp.concatenate([beside[:half] + top.astype(wide), beside[half:]], axis=0)
    far = jnp.concatenate([far[:half], far[half:] + bottom.astype(wide)], axis=0)
    return near, far.astype(low), beside.astype(low)


def team_sum(parts):
    sums = team_sum_core(parts)
    near, far, beside = team_corner_add(sums, *team_corner_hops(sums[3].astype(low)))
    return near + from_chip(far).astype(wide) + from_pair(beside).astype(wide)


def seq_swap(value):
    sent = slots_by_index(value)
    corner = from_core(sent[3])
    came = [sent[0], from_core(sent[1]), from_chip(sent[2]), from_chip(corner)]
    return slots_by_index(jnp.stack(came))


def pair_split(value):
    second = lax.axis_index("fsdp") % 2
    axis = value.ndim - 3
    return [lax.dynamic_index_in_dim(value, which, axis, keepdims=False) for which in (second, 1 - second)]


def pair_add(mine, came):
    return (mine.astype(wide) + came.astype(wide)).astype(low)


def turns_sum(pair):
    size = lax.axis_size("fsdp")
    if size != 8:
        teams = [list(range(w, size, 2)) for w in range(2)]
        return lax.psum_scatter(pair, "fsdp", scatter_dimension=0, axis_index_groups=teams)
    index = lax.axis_index("fsdp")

    def part(by):
        return lax.dynamic_index_in_dim(pair, (index // 2 + by) % (size // 2), 0, keepdims=False)

    total = part(0).astype(wide)
    for by in range(1, size // 2):
        total = total + from_turn(part(by), by).astype(wide)
    return total.astype(low)


def turn(vectors, cosine, sine):
    half = HDIM // 2
    first, second = vectors[:, :half], vectors[:, half:]
    return jnp.concatenate([first * cosine - second * sine, second * cosine + first * sine], axis=1)


def norm_back(grad_hat, normal, inverse):
    return inverse * (grad_hat - normal * jnp.mean(grad_hat * normal, axis=-1, keepdims=True))


def inverse_rms(values):
    return lax.rsqrt(jnp.mean(values * values, axis=-1, keepdims=True) + epsilon)


def local(tokens, gain_attn, w_qkv, w_out, gain_mlp, w_gate_up, w_down, cotangent):
    width = tokens.shape[-1]
    seq_parts = lax.axis_size("seq")
    blocks = lax.axis_size("fsdp")
    assert seq_parts == KVH == 4
    own_tokens = tokens.reshape(-1, width)
    rows = own_tokens.shape[0]
    tile = rows // 2
    slab = rows * seq_parts
    span = SEQ_LEN // slab
    seq_index = lax.axis_index("seq")
    position = lax.axis_index("fsdp") % span
    mirrored = span - 1 - position
    sequences = [list(range(i, i + span)) for i in range(0, blocks, span)]
    groups = None if span == blocks else sequences
    width_q = H * HDIM
    width_kv = KVH * HDIM
    q_part = GROUP * HDIM
    ff_part = FF // seq_parts
    ff_own = -(-ff_part // 256) * 128
    ff_shared = 2 * ff_own - ff_part
    second = lax.axis_index("fsdp") % 2
    teams = [list(range(w, blocks, 2)) for w in range(2)]

    def mirror(half):
        pairs = [(g[i], g[span - 1 - i]) for g in sequences for i in range(span)]
        return lax.ppermute(half, "fsdp", pairs)

    def part(weight, start, step, size=None):
        return lax.dynamic_slice_in_dim(weight, start + seq_index * step, size or step, 1)

    def sc_gather(value):
        return lax.all_gather(value, "fsdp", axis=0, tiled=True)

    def ordered(mine, other, axis):
        first = jnp.where(second == 0, mine, other)
        return jnp.concatenate([first, jnp.where(second == 0, other, mine)], axis=axis)

    def ff_rows(weight, start):
        def columns(which):
            return part(weight, start + which * (ff_own - ff_shared), ff_part, ff_own)

        return ordered(columns(second), from_pair(columns(1 - second)), 0)

    def ff_gather(value):
        return lax.all_gather(value, "fsdp", axis=0, tiled=True, axis_index_groups=teams)

    def ff_sum(value):
        return lax.psum_scatter(value, "fsdp", scatter_dimension=0, tiled=True, axis_index_groups=teams)

    def ff_split(value):
        return pair_split(value.reshape(2, -1, value.shape[1]))

    def ff_columns(mine, other):
        left = jnp.where(second == 0, mine, other)
        right = jnp.where(second == 0, other, mine)
        return jnp.concatenate([left, right[:, ff_shared:]], axis=1)

    def ff_keep(value):
        column = lax.broadcasted_iota(jnp.int32, value.shape, 1)
        return jnp.where(column >= second * ff_shared, value, 0.0).astype(low)

    def gather_halves(halves):
        near, far = (seq_gather(half) for half in halves)
        return jnp.stack([jnp.stack(pair) for pair in zip(near, far, strict=True)]).reshape(slab, width)

    def slots(value):
        return value.astype(low).reshape(-1, rows, value.shape[1])

    kept, sent = own_tokens[:tile], own_tokens[tile:]
    halves = [kept, mirror(sent)]
    inputs_low = jnp.concatenate(halves, axis=0)
    own_feed = cotangent.reshape(-1, width)

    gains = jnp.pad(jnp.stack([gain_attn, gain_mlp], axis=1), ((0, 0), (0, 126)))
    first_part = sc_gather(
        jnp.concatenate(
            [
                part(w_qkv, 0, q_part),
                part(w_qkv, width_q, HDIM),
                part(w_qkv, width_q + width_kv, HDIM),
                gains,
                part(w_out, 0, width // seq_parts),
            ],
            axis=1,
        )
    )
    out_columns = first_part[:, -(width // seq_parts) :]
    qkv_part = first_part[:, : q_part + 2 * HDIM]
    gain_one = first_part[:, q_part + 2 * HDIM].astype(wide)
    gain_two = first_part[:, q_part + 2 * HDIM + 1].astype(wide)

    all_inputs = gather_halves(halves).astype(wide)
    normed_one = lax.optimization_barrier((all_inputs * inverse_rms(all_inputs) * gain_one).astype(low))
    projected = dot(qkv_part, normed_one, 0, 1)
    frequency = 1.0 / 10000.0 ** (jnp.arange(HDIM // 2, dtype=wide) * (2.0 / HDIM))
    row = jnp.arange(slab, dtype=jnp.int32)
    within = (row // rows ^ seq_index) * rows + row % rows
    row_places = jnp.where(row % rows < tile, position, mirrored) * slab + within
    angles = frequency[:, None] * row_places.astype(wide)[None, :]
    cosine, sine = jnp.cos(angles), jnp.sin(angles)
    places = jnp.concatenate([row_places[::tile], seq_index[None].astype(jnp.int32)])
    queries = turn(projected[:q_part].reshape(GROUP, HDIM, slab), cosine, sine) * HDIM**-0.5
    queries = queries.reshape(q_part, slab).astype(low)
    keys_own = turn(projected[q_part : q_part + HDIM].reshape(1, HDIM, slab), cosine, sine)[0]
    kv_own = jnp.concatenate([keys_own, projected[q_part + HDIM :]], axis=0).astype(low)

    kv_own, own_feed, w_gate, w_up, w_down, out_columns = lax.optimization_barrier(
        (kv_own, own_feed, w_gate_up, w_gate_up, w_down, out_columns)
    )
    kv = lax.all_gather(kv_own, "fsdp", axis_index_groups=groups)
    grad_feed_low = jnp.concatenate([own_feed[:tile], mirror(own_feed[tile:])], axis=0)
    out_part = seq_swap(out_columns.reshape(seq_parts, -1, width // seq_parts))
    gate_own, up_own, down_own = ff_rows(w_gate, 0), ff_rows(w_up, FF), ff_rows(w_down, 0)
    gate_own, up_own, down_own, kv, queries, grad_feed_low, out_part = lax.optimization_barrier(
        (gate_own, up_own, down_own, kv, queries, grad_feed_low, out_part)
    )
    out_part = jnp.concatenate(out_part, axis=1)
    gate_part, up_part, down_part = ff_gather(gate_own), ff_gather(up_own), ff_gather(down_own)
    keys, values, keys_t, values_ones = unpack(places, kv, tile)

    tiles = slab // tile // 2
    feed_beside, feed_far = from_pair(grad_feed_low), from_chip(grad_feed_low)
    mixed_far, lse_far = attend(places, queries, keys, values_ones, tile, tiles, tiles)
    mixed_far, feed_beside, feed_far = lax.optimization_barrier((mixed_far, feed_beside, feed_far))
    part_two, part_three = slots(dot(mixed_far.astype(low), out_part, 0, 0))
    branch_far = (part_two.astype(wide) + from_core(part_three).astype(wide)).astype(low)
    branch_far, queries = lax.optimization_barrier((branch_far, queries))
    branch_came = from_chip(branch_far)
    feed_corner = [from_chip(feed_beside[:tile]), from_pair(feed_far[tile:])]
    mixed_near, lse_near = attend(places, queries, keys, values_ones, tile, 0, tiles)
    mixed_near, branch_came, feed_corner = lax.optimization_barrier((mixed_near, branch_came, feed_corner))
    feed_corner = jnp.concatenate(feed_corner, axis=0)
    part_zero, part_one = slots(dot(mixed_near.astype(low), out_part, 0, 0))
    inputs = inputs_low.astype(wide)
    middle = inputs + (
        part_zero.astype(wide) + from_core(part_one).astype(wide) + branch_came.astype(wide)
    )
    inverse_two = inverse_rms(middle)
    hat_two = middle * inverse_two
    normed_two = jnp.concatenate(team_gather((hat_two * gain_two).astype(low)), axis=0)
    grad_feed = jnp.concatenate(
        [each for held in (grad_feed_low, feed_far, feed_beside, feed_corner) for each in (held, from_core(held))],
        axis=0,
    )
    normed_two, grad_feed = lax.optimization_barrier((normed_two, grad_feed))

    gate = jnp.dot(normed_two, gate_part, preferred_element_type=wide)
    up = jnp.dot(normed_two, up_part, preferred_element_type=wide)
    sigmoid = jax.nn.sigmoid(gate)
    silu = gate * sigmoid
    hidden = ff_keep(silu * up)
    grad_hidden = jnp.dot(grad_feed, down_part, preferred_element_type=wide)
    grad_gate = ff_keep(grad_hidden * up * sigmoid * (1.0 + gate * (1.0 - sigmoid)))
    grad_up = ff_keep(grad_hidden * silu)
    product_two = (dot(grad_gate, gate_part, 1, 1) + dot(grad_up, up_part, 1, 1)).astype(low)
    product_two, hidden, grad_gate, grad_up = lax.optimization_barrier(
        (product_two, hidden, grad_gate, grad_up)
    )
    local_down = dot(grad_feed, hidden, 0, 0).astype(low)
    local_gate = dot(normed_two, grad_gate, 0, 0).astype(low)
    local_up = dot(normed_two, grad_up, 0, 0).astype(low)
    feed_sums = team_sum_core(slots(dot(hidden, down_part, 1, 1)))
    grad_normed_two = team_sum(slots(product_two))
    grad_middle = grad_feed_low.astype(wide) + norm_back(
        grad_normed_two * gain_two, hat_two, inverse_two
    )
    sum_down = ff_sum(local_down)
    branch_low, feed_sums, sum_down, local_gate, local_up = lax.optimization_barrier(
        (grad_middle.astype(low), feed_sums, sum_down, local_gate, local_up)
    )
    sum_gate, sum_up = ff_sum(local_gate), ff_sum(local_up)

    back_near = jnp.concatenate([branch_low, from_core(branch_low)], axis=0)
    grads_near = dot(out_part, back_near, 1, 1).astype(low)
    back_come = from_chip(branch_low)
    feed_hops = team_corner_hops(feed_sums[3].astype(low))
    mine_down, theirs = ff_split(sum_down)
    other_down = from_pair(theirs)
    grad_q_near, grad_k, grad_v = attend_back(
        places, queries, grads_near, mixed_near, lse_near, keys, values, keys_t, tile, 0, tiles, slab
    )
    grad_q_near, grad_k, grad_v, back_come, feed_hops, other_down, sum_gate = lax.optimization_barrier(
        (grad_q_near, grad_k, grad_v, back_come, feed_hops, other_down, sum_gate)
    )
    feed_near, feed_far, feed_beside = team_corner_add(feed_sums, *feed_hops)
    own_down = ff_columns(mine_down, other_down)
    mine_gate, theirs_gate = ff_split(sum_gate)
    back_far = jnp.concatenate([back_come, from_core(back_come)], axis=0)
    grads_far = dot(out_part, back_far, 1, 1).astype(low)
    local_out = (
        dot(mixed_near.astype(low), back_near, 1, 0) + dot(mixed_far.astype(low), back_far, 1, 0)
    ).astype(low)
    mine_out, theirs_out = pair_split(local_out.reshape(blocks // 8, 2, -1, width))
    grads_far, theirs_out, feed_far, feed_beside, own_down, theirs_gate = lax.optimization_barrier(
        (grads_far, theirs_out, feed_far, feed_beside, own_down, theirs_gate)
    )
    other_out = from_pair(theirs_out)
    feed_far, feed_beside = from_chip(feed_far), from_pair(feed_beside)
    far_down = from_chip(own_down)
    other_gate = from_pair(theirs_gate)
    grad_q_far, grad_kv = attend_back(
        places, queries, grads_far, mixed_far, lse_far, keys, values, keys_t, tile, tiles, tiles, slab,
        before=(grad_k, grad_v),
    )
    grad_q_far, grad_kv, feed_far, feed_beside, far_down, other_gate, other_out, sum_up = lax.optimization_barrier(
        (grad_q_far, grad_kv, feed_far, feed_beside, far_down, other_gate, other_out, sum_up)
    )
    layer_out = (middle + feed_near + feed_far.astype(wide) + feed_beside.astype(wide)).astype(low)
    out_pair = pair_add(mine_out, other_out).reshape(-1, seq_parts, width // seq_parts)

    grad_kv = lax.psum_scatter(grad_kv, "fsdp", scatter_dimension=0, axis_index_groups=groups)
    grad_q = jnp.concatenate([grad_q_near, grad_q_far], axis=1).astype(low).astype(wide)
    grad_q = turn(grad_q.reshape(GROUP, HDIM, slab), cosine, -sine).reshape(q_part, slab).astype(low)
    mine_q, theirs = pair_split(dot(normed_one, grad_q, 0, 1).astype(low).reshape(blocks // 2, 2, -1, q_part))
    other_q = from_pair(theirs)
    out_swapped = seq_swap(out_pair.transpose(1, 0, 2))
    mirrored_out = mirror(layer_out[tile:])
    down_all = [own_down, from_core(own_down), far_down, from_core(far_down)]
    gate_all = seq_gather(ff_columns(mine_gate, other_gate))
    mine, theirs = ff_split(sum_up)
    up_all = seq_gather(ff_columns(mine, from_pair(theirs)))
    grad_kv, other_q, out_swapped, down_all, gate_all, up_all, mirrored_out = lax.optimization_barrier(
        (grad_kv, other_q, out_swapped, down_all, gate_all, up_all, mirrored_out)
    )
    layer_out = jnp.concatenate([layer_out[:tile], mirrored_out], axis=0)
    grad_q_out_own = ff_sum(
        jnp.concatenate(
            [pair_add(mine_q, other_q).reshape(-1, q_part), jnp.concatenate(out_swapped, axis=0)], axis=1
        )
    )
    grad_k = turn(grad_kv[:HDIM].astype(wide).reshape(1, HDIM, slab), cosine, -sine)[0].astype(low)
    grad_kv = jnp.concatenate([grad_k, grad_kv[HDIM:]], axis=0)
    grad_projected = jnp.concatenate([grad_q, grad_kv], axis=0)
    part_two, part_three = slots(dot(grad_projected[:, slab // 2 :], qkv_part, 0, 1))
    far_one = (part_two.astype(wide) + from_core(part_three).astype(wide)).astype(low)
    far_one, grad_projected, grad_kv = lax.optimization_barrier((far_one, grad_projected, grad_kv))
    came_one = from_chip(far_one)
    part_zero, part_one = slots(dot(grad_projected[:, : slab // 2], qkv_part, 0, 1))
    mine_kv, theirs = pair_split(
        dot(normed_one, grad_kv, 0, 1).astype(low).reshape(blocks // 2, 2, -1, 2 * HDIM)
    )
    other_kv = from_pair(theirs)
    near_one = part_zero.astype(wide) + from_core(part_one).astype(wide)
    near_one, came_one, other_kv = lax.optimization_barrier((near_one, came_one, other_kv))

    grad_normed_one = near_one + came_one.astype(wide)
    inverse_one = inverse_rms(inputs)
    grad_inputs = grad_middle + norm_back(
        grad_normed_one * gain_one, inputs * inverse_one, inverse_one
    )
    grad_inputs, kv_pair = lax.optimization_barrier((grad_inputs, pair_add(mine_kv, other_kv)))
    back = mirror(grad_inputs[tile:].astype(low))
    grad_kv_own = turns_sum(kv_pair)
    own = seq_index[None].astype(jnp.int32)
    weight_grad_gate_up, sums_two = widen_pair(own, gate_all, up_all, w_gate_up)
    weight_grad_down = widen(own, down_all)
    q_out_all = seq_gather(grad_q_out_own)
    back, grad_kv_own, q_out_all, weight_grad_down = lax.optimization_barrier(
        (back, grad_kv_own, q_out_all, weight_grad_down)
    )
    grad_inputs = jnp.concatenate([grad_inputs[:tile], back.astype(wide)], axis=0)

    weight_grad_out = widen(own, q_out_all, 1, width // seq_parts)
    weight_grad_qkv, sums_one = widen_qkv(own, q_out_all, seq_gather(grad_kv_own), w_qkv)
    grad_gain_one = sums_one[:, 0] / gain_attn.astype(wide)
    grad_gain_two = sums_two[:, 0] / gain_mlp.astype(wide)
    return (
        layer_out.reshape(tokens.shape),
        grad_inputs.reshape(tokens.shape),
        weight_grad_qkv,
        weight_grad_out,
        weight_grad_gate_up,
        weight_grad_down,
        grad_gain_one,
        grad_gain_two,
    )


def solution(mesh):
    by_token = P("fsdp", "seq", None)
    by_row = P("fsdp", None)
    return jax.shard_map(
        local,
        mesh=mesh,
        in_specs=(by_token, P("fsdp"), by_row, by_row, P("fsdp"), by_row, by_row, by_token),
        out_specs=(by_token, by_token, by_row, by_row, by_row, by_row, P("fsdp"), P("fsdp")),
        check_vma=False,
    )
```

```python
import functools

import jax
import jax.numpy as jnp
from jax import lax
from jax.experimental import pallas as pl
from jax.experimental.pallas import tpu as pltpu
from jax.sharding import PartitionSpec as P

H = 32
KVH = 4
HDIM = 64
FF = 5632
SEQ_LEN = 8192
GROUP = H // KVH

epsilon = 1e-05
low = jnp.bfloat16
wide = jnp.float32


def dot(left, right, left_dim, right_dim):
    return lax.dot_general(
        left, right, (((left_dim,), (right_dim,)), ((), ())), preferred_element_type=wide
    )


def head_columns(ref, chunk, per_chunk):
    return jnp.concatenate(
        [ref[h * HDIM : (h + 1) * HDIM, :] for h in range(chunk * per_chunk, (chunk + 1) * per_chunk)],
        axis=1,
    )


def causal(offset, first, key_block, tile, copies):
    key_places = offset + lax.broadcasted_iota(jnp.int32, (key_block, tile), 0)
    query_places = first + lax.broadcasted_iota(jnp.int32, (key_block, tile), 1)
    return jnp.concatenate([key_places <= query_places] * copies, axis=1)


def each_piece(places, span, tiles, tile, visit):
    own = places[tiles]

    def one(n, _):
        block, rest = n // tiles, n % tiles
        index, half = rest // 2, rest % 2
        sender = jnp.where(half == 0, block, span - 1 - block)
        visit(
            sender,
            pl.multiple_of(((index ^ own) * 2 + half) * tile, tile),
            pl.multiple_of(n * tile, tile),
        )
        return 0

    lax.fori_loop(0, span * tiles, one, 0, unroll=8)


def unpack_kernel(places, kv_ref, keys_ref, values_ref, kt_ref, ones_ref, *, tile, tiles):
    ones_ref[HDIM:, :] = jnp.ones((8, ones_ref.shape[1]), low)

    def visit(sender, start, place):
        piece = kv_ref[sender, :, pl.ds(start, tile)]
        kt_ref[:, pl.ds(place, tile)] = piece[:HDIM]
        ones_ref[:HDIM, pl.ds(place, tile)] = piece[HDIM:]
        turned = piece.astype(wide).T.astype(low)
        keys_ref[pl.ds(place, tile), :] = turned[:, :HDIM]
        values_ref[pl.ds(place, tile), :] = turned[:, HDIM:]

    each_piece(places, kv_ref.shape[0], tiles, tile, visit)


def whole_block(shape):
    return pl.BlockSpec(shape, lambda i, p: (0,) * len(shape))


def unpack(places, kv, tile):
    span, _, slab = kv.shape
    length = span * slab
    shapes = [(length, HDIM), (length, HDIM), (HDIM, length), (HDIM + 8, length)]
    return pl.pallas_call(
        functools.partial(unpack_kernel, tile=tile, tiles=slab // tile),
        grid_spec=pltpu.PrefetchScalarGridSpec(
            num_scalar_prefetch=1,
            grid=(1,),
            in_specs=[whole_block(kv.shape)],
            out_specs=[whole_block(shape) for shape in shapes],
        ),
        out_shape=[jax.ShapeDtypeStruct(shape, low) for shape in shapes],
        compiler_params=pltpu.CompilerParams(vmem_limit_bytes=32 << 20),
        name="unpack",
    )(places, kv)


def attend_kernel(places, q_ref, keys_ref, values_ref, mixed_ref, lse_ref, max_s, sum_s, *, key_block, per_chunk, base):
    tile = q_ref.shape[1]
    chunks = GROUP // per_chunk
    first = places[pl.program_id(0) + base]
    queries = [head_columns(q_ref, c, per_chunk) for c in range(chunks)]
    max_s[...] = jnp.full(max_s.shape, -1e30, wide)
    sum_s[...] = jnp.zeros(sum_s.shape, wide)

    def step(index, masked=0):
        offset = pl.multiple_of(index * key_block, key_block)
        size = masked or key_block
        keys = keys_ref[pl.ds(offset, size), :]
        values = values_ref[:, pl.ds(offset, size)]
        if masked:
            keep = causal(offset, first, size, tile, per_chunk)
        for c in range(chunks):
            scores = jnp.dot(keys, queries[c], preferred_element_type=wide)
            if masked:
                scores = jnp.where(keep, scores, -1e30)
            old = max_s[c]
            new = jnp.maximum(old, jnp.max(scores, axis=0, keepdims=True))
            probs = jnp.exp(scores - new).astype(low)
            max_s[c] = new
            sum_s[c] = sum_s[c] * jnp.exp(old - new) + jnp.dot(
                values, probs, preferred_element_type=wide
            )

    full = first // key_block
    lax.fori_loop(0, full, lambda i, _: (step(i), 0)[1], 0)
    for size in range(tile, key_block + tile, tile):

        @pl.when(first % key_block == size - tile)
        def _(size=size):
            step(full, size)

    for c in range(chunks):
        sums = sum_s[c]
        total = sums[HDIM : HDIM + 1, :]
        mixed = sums[:HDIM, :] * (1.0 / total)
        lse = max_s[c] + jnp.log(total)
        for i in range(per_chunk):
            h = c * per_chunk + i
            mixed_ref[h * HDIM : (h + 1) * HDIM, :] = mixed[:, i * tile : (i + 1) * tile]
            lse_ref[0, h : h + 1, :] = lse[:, i * tile : (i + 1) * tile]


def attend(places, queries, keys, values_ones, tile, base, tiles, key_block=512, per_chunk=8):
    features, _ = queries.shape
    length = keys.shape[0]
    chunks = GROUP // per_chunk
    pairs = GROUP * tiles * tile * length // 2
    return pl.pallas_call(
        functools.partial(attend_kernel, key_block=key_block, per_chunk=per_chunk, base=base),
        grid_spec=pltpu.PrefetchScalarGridSpec(
            num_scalar_prefetch=1,
            grid=(tiles,),
            in_specs=[
                pl.BlockSpec((features, tile), lambda i, p: (0, i + base)),
                whole_block(keys.shape),
                whole_block(values_ones.shape),
            ],
            out_specs=[
                pl.BlockSpec((features, tile), lambda i, p: (0, i)),
                pl.BlockSpec((1, GROUP, tile), lambda i, p: (i, 0, 0)),
            ],
            scratch_shapes=[
                pltpu.VMEM((chunks, 1, per_chunk * tile), wide),
                pltpu.VMEM((chunks, HDIM + 8, per_chunk * tile), wide),
            ],
        ),
        out_shape=[
            jax.ShapeDtypeStruct((features, tiles * tile), wide),
            jax.ShapeDtypeStruct((tiles, GROUP, tile), wide),
        ],
        compiler_params=pltpu.CompilerParams(vmem_limit_bytes=40 << 20),
        cost_estimate=pl.CostEstimate(
            flops=pairs * HDIM * 16, bytes_accessed=8 << 20, transcendentals=pairs
        ),
        name="attend",
    )(places, queries, keys, values_ones)


def attend_back_kernel(places, *refs, key_block, per_chunk, base, tiles, slab, last):
    q_ref, g_ref, mixed_ref, lse_ref, keys_ref, values_ref, kt_ref = refs[:7]
    if last:
        k_before, v_before, gq_ref, gkv_ref, gq_s, gk_s, gv_s = refs[7:]
    else:
        gq_ref, gk_s, gv_s, gq_s = refs[7:]
    tile = q_ref.shape[1]
    chunks = GROUP // per_chunk
    first = places[pl.program_id(0) + base]

    @pl.when(pl.program_id(0) == 0)
    def _():
        gk_s[...] = k_before[...] if last else jnp.zeros(gk_s.shape, wide)
        gv_s[...] = v_before[...] if last else jnp.zeros(gv_s.shape, wide)

    queries = [head_columns(q_ref, c, per_chunk) for c in range(chunks)]
    grads = [head_columns(g_ref, c, per_chunk) for c in range(chunks)]
    inner = [
        jnp.sum(grads[c].astype(wide) * head_columns(mixed_ref, c, per_chunk), axis=0, keepdims=True)
        for c in range(chunks)
    ]
    lse = [
        jnp.concatenate([lse_ref[0, c * per_chunk + i : c * per_chunk + i + 1, :] for i in range(per_chunk)], axis=1)
        for c in range(chunks)
    ]
    gq_s[...] = jnp.zeros(gq_s.shape, wide)

    def step(index, masked=0):
        offset = pl.multiple_of(index * key_block, key_block)
        size = masked or key_block
        keys = keys_ref[pl.ds(offset, size), :]
        values = values_ref[pl.ds(offset, size), :]
        keys_t = kt_ref[:, pl.ds(offset, size)]
        if masked:
            keep = causal(offset, first, size, tile, per_chunk)
        grad_k = grad_v = None
        for c in range(chunks):
            scores = jnp.dot(keys, queries[c], preferred_element_type=wide)
            if masked:
                scores = jnp.where(keep, scores, -1e30)
            probs = jnp.exp(scores - lse[c])
            grad_probs = jnp.dot(values, grads[c], preferred_element_type=wide)
            grad_scores = (probs * (grad_probs - inner[c])).astype(low)
            more_k = dot(grad_scores, queries[c], 1, 1)
            more_v = dot(probs.astype(low), grads[c], 1, 1)
            gq_s[c] += jnp.dot(keys_t, grad_scores, preferred_element_type=wide)
            grad_k = more_k if grad_k is None else grad_k + more_k
            grad_v = more_v if grad_v is None else grad_v + more_v
        gk_s[pl.ds(offset, size), :] += grad_k
        gv_s[pl.ds(offset, size), :] += grad_v

    full = first // key_block
    lax.fori_loop(0, full, lambda i, _: (step(i), 0)[1], 0)
    for size in range(tile, key_block + tile, tile):

        @pl.when(first % key_block == size - tile)
        def _(size=size):
            step(full, size)

    for c in range(chunks):
        grad_q = gq_s[c] * HDIM**-0.5
        for i in range(per_chunk):
            h = c * per_chunk + i
            gq_ref[h * HDIM : (h + 1) * HDIM, :] = grad_q[:, i * tile : (i + 1) * tile]

    if last:

        @pl.when(pl.program_id(0) == tiles - 1)
        def _():
            def visit(sender, start, place):
                both = jnp.concatenate([gk_s[pl.ds(place, tile), :], gv_s[pl.ds(place, tile), :]], axis=1)
                gkv_ref[sender, :, pl.ds(start, tile)] = both.T.astype(low)

            each_piece(places, gkv_ref.shape[0], slab // tile, tile, visit)


def attend_back(
    places, queries, grads, mixed, lse, keys, values, keys_t, tile, base, tiles, slab, before=None,
    key_block=512, per_chunk=8,
):
    features, _ = queries.shape
    length = keys.shape[0]
    span = length // slab
    chunks = GROUP // per_chunk
    pairs = GROUP * tiles * tile * length // 2
    last = before is not None
    by_tile = pl.BlockSpec((features, tile), lambda i, p: (0, i))
    packed = (span, 2 * HDIM, slab)
    sums = [pltpu.VMEM((length, HDIM), wide)] * 2
    return pl.pallas_call(
        functools.partial(
            attend_back_kernel,
            key_block=key_block, per_chunk=per_chunk, base=base, tiles=tiles, slab=slab, last=last,
        ),
        grid_spec=pltpu.PrefetchScalarGridSpec(
            num_scalar_prefetch=1,
            grid=(tiles,),
            in_specs=[
                pl.BlockSpec((features, tile), lambda i, p: (0, i + base)),
                by_tile,
                by_tile,
                pl.BlockSpec((1, GROUP, tile), lambda i, p: (i, 0, 0)),
                whole_block(keys.shape),
                whole_block(values.shape),
                whole_block(keys_t.shape),
            ]
            + [whole_block(keys.shape)] * (2 * last),
            out_specs=[by_tile] + ([whole_block(packed)] if last else [whole_block(keys.shape)] * 2),
            scratch_shapes=[pltpu.VMEM((chunks, HDIM, per_chunk * tile), wide)] + sums * last,
        ),
        out_shape=[jax.ShapeDtypeStruct((features, tiles * tile), wide)]
        + ([jax.ShapeDtypeStruct(packed, low)] if last else [jax.ShapeDtypeStruct(keys.shape, wide)] * 2),
        compiler_params=pltpu.CompilerParams(vmem_limit_bytes=56 << 20),
        cost_estimate=pl.CostEstimate(
            flops=pairs * HDIM * 40, bytes_accessed=16 << 20, transcendentals=pairs
        ),
        name="attend_back",
    )(places, queries, grads, mixed, lse, keys, values, keys_t, *(before or ()))


def widen_kernel(own, *refs):
    out_ref = refs[-1]
    for i, ref in enumerate(refs[:-1]):

        @pl.when(pl.program_id(0) == i)
        def _(ref=ref):
            out_ref[...] = ref[...].astype(wide)


def widen(own, pieces):
    parts = len(pieces)
    rows, columns = pieces[0].shape
    return pl.pallas_call(
        widen_kernel,
        grid_spec=pltpu.PrefetchScalarGridSpec(
            num_scalar_prefetch=1,
            grid=(parts,),
            in_specs=[pl.BlockSpec((rows, columns), lambda i, own: (0, 0))] * parts,
            out_specs=pl.BlockSpec((rows, columns), lambda i, own: (0, i ^ own[0])),
        ),
        out_shape=jax.ShapeDtypeStruct((rows, parts * columns), wide),
        compiler_params=pltpu.CompilerParams(vmem_limit_bytes=24 << 20),
        name="widen",
    )(own, *pieces)


def widen_half_kernel(own, *refs, parts):
    weight_ref, (out_ref, total_ref) = refs[parts], refs[-2:]
    step = pl.program_id(0)
    for i, ref in enumerate(refs[:parts]):

        @pl.when(step == i)
        def _(ref=ref):
            value = ref[...].astype(wide)
            out_ref[...] = value
            more = jnp.sum(value * weight_ref[...].astype(wide), axis=1, keepdims=True)
            total_ref[...] = jnp.where(step == 0, more, total_ref[...] + more)


def widen_half(own, pieces, weight, half, before=()):
    parts = len(pieces)
    rows, columns = pieces[0].shape

    def place(i, own):
        return (0, half * parts + (i ^ own[0]))

    return pl.pallas_call(
        functools.partial(widen_half_kernel, parts=parts),
        grid_spec=pltpu.PrefetchScalarGridSpec(
            num_scalar_prefetch=1,
            grid=(parts,),
            in_specs=[pl.BlockSpec((rows, columns), lambda i, own: (0, 0))] * parts
            + [pl.BlockSpec((rows, columns), place)]
            + [pl.BlockSpec(memory_space=pl.ANY)] * len(before),
            out_specs=[
                pl.BlockSpec((rows, columns), place),
                pl.BlockSpec((rows, 1), lambda i, own: (0, 0)),
            ],
        ),
        out_shape=[
            jax.ShapeDtypeStruct((rows, 2 * parts * columns), wide),
            jax.ShapeDtypeStruct((rows, 1), wide),
        ],
        input_output_aliases={parts + 2: 0} if before else {},
        compiler_params=pltpu.CompilerParams(vmem_limit_bytes=32 << 20),
        name="widen_half",
    )(own, *pieces, weight, *before)


def widen_qkv_kernel(own, *refs, parts):
    weight_ref, out_ref, total_ref = refs[-3:]
    step = pl.program_id(0)

    def write(value):
        out_ref[...] = value
        more = jnp.sum(value * weight_ref[...].astype(wide), axis=1, keepdims=True)
        total_ref[...] = jnp.where(step == 0, more, total_ref[...] + more)

    for i, ref in enumerate(refs[:parts]):

        @pl.when(step == i)
        def _(ref=ref):
            write(ref[...].astype(wide))

    @pl.when(step == parts)
    def _():
        pieces = [ref[...].astype(wide) for ref in refs[parts : 2 * parts]]
        ordered = []
        for i in range(parts):
            value = pieces[i]
            for j in range(1, parts):
                value = jnp.where(own[0] == j, pieces[i ^ j], value)
            ordered.append(value)
        write(jnp.concatenate([v[:, :HDIM] for v in ordered] + [v[:, HDIM:] for v in ordered], axis=1))


def widen_qkv(own, queries, rest, weight):
    parts = len(queries)
    rows, columns = queries[0].shape[0], parts * 2 * HDIM

    def place(i, own):
        return (0, jnp.where(i < parts, i ^ own[0], parts))

    return pl.pallas_call(
        functools.partial(widen_qkv_kernel, parts=parts),
        grid_spec=pltpu.PrefetchScalarGridSpec(
            num_scalar_prefetch=1,
            grid=(parts + 1,),
            in_specs=[pl.BlockSpec((rows, columns), lambda i, own: (0, 0))] * parts
            + [pl.BlockSpec((rows, 2 * HDIM), lambda i, own: (0, 0))] * parts
            + [pl.BlockSpec((rows, columns), place)],
            out_specs=[
                pl.BlockSpec((rows, columns), place),
                pl.BlockSpec((rows, 1), lambda i, own: (0, 0)),
            ],
        ),
        out_shape=[
            jax.ShapeDtypeStruct((rows, (parts + 1) * columns), wide),
            jax.ShapeDtypeStruct((rows, 1), wide),
        ],
        compiler_params=pltpu.CompilerParams(vmem_limit_bytes=24 << 20),
        name="widen_qkv",
    )(own, *queries, *rest, weight)


def from_core(value):
    return lax.ppermute(value, "seq", [(i, i ^ 1) for i in range(lax.axis_size("seq"))])


def from_chip(value):
    return lax.ppermute(value, "seq", [(i, i ^ 2) for i in range(lax.axis_size("seq"))])


def seq_gather(value):
    far = from_chip(value)
    return [value, from_core(value), far, from_core(far)]


def seq_sum_core(parts):
    far = parts[2].astype(wide) + from_core(parts[3]).astype(wide)
    near = parts[0].astype(wide) + from_core(parts[1]).astype(wide)
    return near, far.astype(low)


def seq_sum(parts):
    near, far = seq_sum_core(parts)
    return near + from_chip(far).astype(wide)


def slots_by_index(value):
    own = lax.axis_index("seq")
    return [
        lax.dynamic_index_in_dim(value, own ^ j, 0, keepdims=False) for j in range(lax.axis_size("seq"))
    ]


def from_turn(value, by):
    size = lax.axis_size("fsdp")
    return lax.ppermute(value, "fsdp", [(i, (i + 2 * by) % size) for i in range(size)])


def from_pair(value):
    return lax.ppermute(value, "fsdp", [(i, i ^ 1) for i in range(lax.axis_size("fsdp"))])


def team_gather(value):
    half = value.shape[0] // 2
    beside, far = from_pair(value), from_chip(value)
    corner = jnp.concatenate([from_chip(beside[:half]), from_pair(far[half:])], axis=0)
    return [each for held in (value, far, beside, corner) for each in (held, from_core(held))]


def team_sum_core(parts):
    return [
        parts[i].astype(wide) + from_core(parts[i + 1]).astype(wide) for i in range(0, len(parts), 2)
    ]


def team_corner_hops(corner):
    half = corner.shape[0] // 2
    return from_chip(corner[:half]), from_pair(corner[half:])


def team_corner_add(sums, top, bottom):
    near, far, beside, _ = sums
    half = near.shape[0] // 2
    beside = jnp.concatenate([beside[:half] + top.astype(wide), beside[half:]], axis=0)
    far = jnp.concatenate([far[:half], far[half:] + bottom.astype(wide)], axis=0)
    return near, far.astype(low), beside.astype(low)


def team_sum(parts):
    sums = team_sum_core(parts)
    near, far, beside = team_corner_add(sums, *team_corner_hops(sums[3].astype(low)))
    return near + from_chip(far).astype(wide) + from_pair(beside).astype(wide)


def from_diagonal(value):
    return lax.ppermute(value, "seq", [(i, i ^ 3) for i in range(lax.axis_size("seq"))])


def seq_swap(value):
    sent = slots_by_index(value)
    came = [sent[0], from_core(sent[1]), from_chip(sent[2]), from_diagonal(sent[3])]
    return slots_by_index(jnp.stack(came))


def pair_split(value):
    second = lax.axis_index("fsdp") % 2
    axis = value.ndim - 3
    return [lax.dynamic_index_in_dim(value, which, axis, keepdims=False) for which in (second, 1 - second)]


def pair_add(mine, came):
    return (mine.astype(wide) + came.astype(wide)).astype(low)


def turns_sum(pair):
    size = lax.axis_size("fsdp")
    if size != 8:
        teams = [list(range(w, size, 2)) for w in range(2)]
        return lax.psum_scatter(pair, "fsdp", scatter_dimension=0, axis_index_groups=teams)
    index = lax.axis_index("fsdp")

    def part(by):
        return lax.dynamic_index_in_dim(pair, (index // 2 + by) % (size // 2), 0, keepdims=False)

    total = part(0).astype(wide)
    for by in range(1, size // 2):
        total = total + from_turn(part(by), by).astype(wide)
    return total.astype(low)


def turn(vectors, cosine, sine):
    half = HDIM // 2
    first, second = vectors[:, :half], vectors[:, half:]
    return jnp.concatenate([first * cosine - second * sine, second * cosine + first * sine], axis=1)


def norm_back(grad_hat, normal, inverse):
    return inverse * (grad_hat - normal * jnp.mean(grad_hat * normal, axis=-1, keepdims=True))


def inverse_rms(values):
    return lax.rsqrt(jnp.mean(values * values, axis=-1, keepdims=True) + epsilon)


def local(tokens, gain_attn, w_qkv, w_out, gain_mlp, w_gate_up, w_down, cotangent):
    width = tokens.shape[-1]
    seq_parts = lax.axis_size("seq")
    blocks = lax.axis_size("fsdp")
    assert seq_parts == KVH == 4
    own_tokens = tokens.reshape(-1, width)
    rows = own_tokens.shape[0]
    tile = rows // 2
    slab = rows * seq_parts
    span = SEQ_LEN // slab
    seq_index = lax.axis_index("seq")
    position = lax.axis_index("fsdp") % span
    mirrored = span - 1 - position
    sequences = [list(range(i, i + span)) for i in range(0, blocks, span)]
    groups = None if span == blocks else sequences
    width_q = H * HDIM
    width_kv = KVH * HDIM
    q_part = GROUP * HDIM
    ff_part = FF // seq_parts
    ff_own = -(-ff_part // 256) * 128
    ff_shared = 2 * ff_own - ff_part
    second = lax.axis_index("fsdp") % 2
    teams = [list(range(w, blocks, 2)) for w in range(2)]

    def mirror(half):
        pairs = [(g[i], g[span - 1 - i]) for g in sequences for i in range(span)]
        return lax.ppermute(half, "fsdp", pairs)

    def part(weight, start, step, size=None):
        return lax.dynamic_slice_in_dim(weight, start + seq_index * step, size or step, 1)

    def sc_gather(value):
        return lax.all_gather(value, "fsdp", axis=0, tiled=True)

    def ordered(mine, other, axis):
        first = jnp.where(second == 0, mine, other)
        return jnp.concatenate([first, jnp.where(second == 0, other, mine)], axis=axis)

    def ff_rows(weight, start):
        def columns(which):
            return part(weight, start + which * (ff_own - ff_shared), ff_part, ff_own)

        return ordered(columns(second), from_pair(columns(1 - second)), 0)

    def ff_gather(value):
        return lax.all_gather(value, "fsdp", axis=0, tiled=True, axis_index_groups=teams)

    def ff_sum(value):
        return lax.psum_scatter(value, "fsdp", scatter_dimension=0, tiled=True, axis_index_groups=teams)

    def ff_split(value):
        return pair_split(value.reshape(2, -1, value.shape[1]))

    def ff_columns(mine, other):
        left = jnp.where(second == 0, mine, other)
        right = jnp.where(second == 0, other, mine)
        return jnp.concatenate([left, right[:, ff_shared:]], axis=1)

    def ff_keep(value):
        column = lax.broadcasted_iota(jnp.int32, value.shape, 1)
        return jnp.where(column >= second * ff_shared, value, 0.0).astype(low)

    def gather_halves(halves):
        near, far = (seq_gather(half) for half in halves)
        return jnp.stack([jnp.stack(pair) for pair in zip(near, far, strict=True)]).reshape(slab, width)

    def slots(value):
        return value.astype(low).reshape(-1, rows, value.shape[1])

    kept, sent = own_tokens[:tile], own_tokens[tile:]
    halves = [kept, mirror(sent)]
    inputs_low = jnp.concatenate(halves, axis=0)
    own_feed = cotangent.reshape(-1, width)

    gains = jnp.pad(jnp.stack([gain_attn, gain_mlp], axis=1), ((0, 0), (0, 126)))
    first_part = sc_gather(
        jnp.concatenate(
            [
                part(w_qkv, 0, q_part),
                part(w_qkv, width_q, HDIM),
                part(w_qkv, width_q + width_kv, HDIM),
                gains,
                part(w_out, 0, width // seq_parts),
            ],
            axis=1,
        )
    )
    out_columns = first_part[:, -(width // seq_parts) :]
    qkv_part = first_part[:, : q_part + 2 * HDIM]
    gain_one = first_part[:, q_part + 2 * HDIM].astype(wide)
    gain_two = first_part[:, q_part + 2 * HDIM + 1].astype(wide)

    all_inputs = gather_halves(halves).astype(wide)
    normed_one = lax.optimization_barrier((all_inputs * inverse_rms(all_inputs) * gain_one).astype(low))
    projected = dot(qkv_part, normed_one, 0, 1)
    frequency = 1.0 / 10000.0 ** (jnp.arange(HDIM // 2, dtype=wide) * (2.0 / HDIM))
    row = jnp.arange(slab, dtype=jnp.int32)
    within = (row // rows ^ seq_index) * rows + row % rows
    row_places = jnp.where(row % rows < tile, position, mirrored) * slab + within
    angles = frequency[:, None] * row_places.astype(wide)[None, :]
    cosine, sine = jnp.cos(angles), jnp.sin(angles)
    places = jnp.concatenate([row_places[::tile], seq_index[None].astype(jnp.int32)])
    queries = turn(projected[:q_part].reshape(GROUP, HDIM, slab), cosine, sine) * HDIM**-0.5
    queries = queries.reshape(q_part, slab).astype(low)
    keys_own = turn(projected[q_part : q_part + HDIM].reshape(1, HDIM, slab), cosine, sine)[0]
    kv_own = jnp.concatenate([keys_own, projected[q_part + HDIM :]], axis=0).astype(low)

    kv_own, own_feed, w_gate, w_up, w_down, out_columns = lax.optimization_barrier(
        (kv_own, own_feed, w_gate_up, w_gate_up, w_down, out_columns)
    )
    kv = lax.all_gather(kv_own, "fsdp", axis_index_groups=groups)
    grad_feed_low = jnp.concatenate([own_feed[:tile], mirror(own_feed[tile:])], axis=0)
    out_part = seq_swap(out_columns.reshape(seq_parts, -1, width // seq_parts))
    gate_own, up_own, down_own = ff_rows(w_gate, 0), ff_rows(w_up, FF), ff_rows(w_down, 0)
    gate_own, up_own, down_own, kv, queries, grad_feed_low, out_part = lax.optimization_barrier(
        (gate_own, up_own, down_own, kv, queries, grad_feed_low, out_part)
    )
    out_part = jnp.concatenate(out_part, axis=1)
    gate_part, up_part, down_part = ff_gather(gate_own), ff_gather(up_own), ff_gather(down_own)
    keys, values, keys_t, values_ones = unpack(places, kv, tile)

    tiles = slab // tile // 2
    feed_beside, feed_far = from_pair(grad_feed_low), from_chip(grad_feed_low)
    mixed_far, lse_far = attend(places, queries, keys, values_ones, tile, tiles, tiles)
    mixed_far, feed_beside, feed_far = lax.optimization_barrier((mixed_far, feed_beside, feed_far))
    part_two, part_three = slots(dot(mixed_far.astype(low), out_part, 0, 0))
    branch_far = (part_two.astype(wide) + from_core(part_three).astype(wide)).astype(low)
    branch_far, queries = lax.optimization_barrier((branch_far, queries))
    branch_came = from_chip(branch_far)
    feed_corner = [from_chip(feed_beside[:tile]), from_pair(feed_far[tile:])]
    mixed_near, lse_near = attend(places, queries, keys, values_ones, tile, 0, tiles)
    mixed_near, branch_came, feed_corner = lax.optimization_barrier((mixed_near, branch_came, feed_corner))
    feed_corner = jnp.concatenate(feed_corner, axis=0)
    part_zero, part_one = slots(dot(mixed_near.astype(low), out_part, 0, 0))
    inputs = inputs_low.astype(wide)
    middle = inputs + (
        part_zero.astype(wide) + from_core(part_one).astype(wide) + branch_came.astype(wide)
    )
    inverse_two = inverse_rms(middle)
    hat_two = middle * inverse_two
    normed_two = jnp.concatenate(team_gather((hat_two * gain_two).astype(low)), axis=0)
    grad_feed = jnp.concatenate(
        [each for held in (grad_feed_low, feed_far, feed_beside, feed_corner) for each in (held, from_core(held))],
        axis=0,
    )
    normed_two, grad_feed = lax.optimization_barrier((normed_two, grad_feed))

    gate = jnp.dot(normed_two, gate_part, preferred_element_type=wide)
    up = jnp.dot(normed_two, up_part, preferred_element_type=wide)
    sigmoid = jax.nn.sigmoid(gate)
    silu = gate * sigmoid
    hidden = ff_keep(silu * up)
    grad_hidden = jnp.dot(grad_feed, down_part, preferred_element_type=wide)
    grad_gate = ff_keep(grad_hidden * up * sigmoid * (1.0 + gate * (1.0 - sigmoid)))
    grad_up = ff_keep(grad_hidden * silu)
    product_two = (dot(grad_gate, gate_part, 1, 1) + dot(grad_up, up_part, 1, 1)).astype(low)
    product_two, hidden, grad_gate, grad_up = lax.optimization_barrier(
        (product_two, hidden, grad_gate, grad_up)
    )
    local_down = dot(grad_feed, hidden, 0, 0).astype(low)
    local_gate = dot(normed_two, grad_gate, 0, 0).astype(low)
    local_up = dot(normed_two, grad_up, 0, 0).astype(low)
    feed_sums = team_sum_core(slots(dot(hidden, down_part, 1, 1)))
    grad_normed_two = team_sum(slots(product_two))
    grad_middle = grad_feed_low.astype(wide) + norm_back(
        grad_normed_two * gain_two, hat_two, inverse_two
    )
    sum_down = ff_sum(local_down)
    branch_low, feed_sums, sum_down, local_gate, local_up = lax.optimization_barrier(
        (grad_middle.astype(low), feed_sums, sum_down, local_gate, local_up)
    )
    sum_gate, sum_up = ff_sum(local_gate), ff_sum(local_up)

    back_near = jnp.concatenate([branch_low, from_core(branch_low)], axis=0)
    grads_near = dot(out_part, back_near, 1, 1).astype(low)
    back_come = from_chip(branch_low)
    feed_hops = team_corner_hops(feed_sums[3].astype(low))
    mine_down, theirs = ff_split(sum_down)
    other_down = from_pair(theirs)
    grad_q_near, grad_k, grad_v = attend_back(
        places, queries, grads_near, mixed_near, lse_near, keys, values, keys_t, tile, 0, tiles, slab
    )
    grad_q_near, grad_k, grad_v, back_come, feed_hops, other_down, sum_gate = lax.optimization_barrier(
        (grad_q_near, grad_k, grad_v, back_come, feed_hops, other_down, sum_gate)
    )
    feed_near, feed_far, feed_beside = team_corner_add(feed_sums, *feed_hops)
    own_down = ff_columns(mine_down, other_down)
    mine_gate, theirs_gate = ff_split(sum_gate)
    back_far = jnp.concatenate([back_come, from_core(back_come)], axis=0)
    grads_far = dot(out_part, back_far, 1, 1).astype(low)
    local_out = (
        dot(mixed_near.astype(low), back_near, 1, 0) + dot(mixed_far.astype(low), back_far, 1, 0)
    ).astype(low)
    mine_out, theirs_out = pair_split(local_out.reshape(blocks // 8, 2, -1, width))
    grads_far, theirs_out, feed_far, feed_beside, own_down, theirs_gate = lax.optimization_barrier(
        (grads_far, theirs_out, feed_far, feed_beside, own_down, theirs_gate)
    )
    other_out = from_pair(theirs_out)
    feed_far, feed_beside = from_chip(feed_far), from_pair(feed_beside)
    far_down = from_chip(own_down)
    other_gate = from_pair(theirs_gate)
    grad_q_far, grad_kv = attend_back(
        places, queries, grads_far, mixed_far, lse_far, keys, values, keys_t, tile, tiles, tiles, slab,
        before=(grad_k, grad_v),
    )
    grad_q_far, grad_kv, feed_far, feed_beside, far_down, other_gate, other_out, sum_up = lax.optimization_barrier(
        (grad_q_far, grad_kv, feed_far, feed_beside, far_down, other_gate, other_out, sum_up)
    )
    layer_out = (middle + feed_near + feed_far.astype(wide) + feed_beside.astype(wide)).astype(low)

    grad_kv = lax.psum_scatter(grad_kv, "fsdp", scatter_dimension=0, axis_index_groups=groups)
    grad_q = jnp.concatenate([grad_q_near, grad_q_far], axis=1).astype(low).astype(wide)
    grad_q = turn(grad_q.reshape(GROUP, HDIM, slab), cosine, -sine).reshape(q_part, slab).astype(low)
    own = seq_index[None].astype(jnp.int32)
    mine_q, theirs = pair_split(dot(normed_one, grad_q, 0, 1).astype(low).reshape(blocks // 2, 2, -1, q_part))
    other_q = from_pair(theirs)
    out_pair = pair_add(mine_out, other_out).reshape(-1, seq_parts, width // seq_parts)
    out_sums = seq_swap(out_pair.transpose(1, 0, 2))
    down_all = [own_down, from_core(own_down), far_down, from_core(far_down)]
    gate_all = seq_gather(ff_columns(mine_gate, other_gate))
    mine, theirs = ff_split(sum_up)
    up_all = seq_gather(ff_columns(mine, from_pair(theirs)))
    q_far = dot(grad_q[:, slab // 2 :], qkv_part[:, :q_part], 0, 1)
    q_near = dot(grad_q[:, : slab // 2], qkv_part[:, :q_part], 0, 1)
    sent_out = layer_out[tile:]
    grad_kv, other_q, out_sums, down_all, gate_all, up_all, sent_out, q_far, q_near = lax.optimization_barrier(
        (grad_kv, other_q, out_sums, down_all, gate_all, up_all, sent_out, q_far, q_near)
    )
    grad_k = turn(grad_kv[:HDIM].astype(wide).reshape(1, HDIM, slab), cosine, -sine)[0].astype(low)
    grad_kv = jnp.concatenate([grad_k, grad_kv[HDIM:]], axis=0)
    part_two, part_three = slots(q_far + dot(grad_kv[:, slab // 2 :], qkv_part[:, q_part:], 0, 1))
    far_one = (part_two.astype(wide) + from_core(part_three).astype(wide)).astype(low)
    far_one, grad_kv, q_near, mine_q, other_q, out_sums = lax.optimization_barrier(
        (far_one, grad_kv, q_near, mine_q, other_q, out_sums)
    )
    came_one = from_chip(far_one)
    grad_out_own = ff_sum(jnp.concatenate(out_sums, axis=0))
    grad_q_own = ff_sum(pair_add(mine_q, other_q).reshape(-1, q_part))
    part_zero, part_one = slots(q_near + dot(grad_kv[:, : slab // 2], qkv_part[:, q_part:], 0, 1))
    weight_grad_down = widen(own, down_all)
    weight_grad_gate, sums_gate = widen_half(own, gate_all, w_gate_up, 0)
    weight_grad_gate_up, sums_up = widen_half(own, up_all, w_gate_up, 1, (weight_grad_gate,))
    mine_kv, theirs = pair_split(
        dot(normed_one, grad_kv, 0, 1).astype(low).reshape(blocks // 2, 2, -1, 2 * HDIM)
    )
    other_kv = from_pair(theirs)
    near_one = part_zero.astype(wide) + from_core(part_one).astype(wide)
    near_one, came_one, other_kv = lax.optimization_barrier((near_one, came_one, other_kv))

    grad_normed_one = near_one + came_one.astype(wide)
    inverse_one = inverse_rms(inputs)
    grad_inputs = grad_middle + norm_back(
        grad_normed_one * gain_one, inputs * inverse_one, inverse_one
    )
    grad_inputs, kv_pair = lax.optimization_barrier((grad_inputs, pair_add(mine_kv, other_kv)))
    back = mirror(grad_inputs[tile:].astype(low))
    grad_kv_own = turns_sum(kv_pair)
    back, grad_kv_own, grad_q_own, grad_out_own, sent_out, weight_grad_gate_up, weight_grad_down = (
        lax.optimization_barrier(
            (back, grad_kv_own, grad_q_own, grad_out_own, sent_out, weight_grad_gate_up, weight_grad_down)
        )
    )
    layer_out = jnp.concatenate([layer_out[:tile], mirror(sent_out)], axis=0)
    q_all, out_all = seq_gather(grad_q_own), seq_gather(grad_out_own)
    grad_inputs = jnp.concatenate([grad_inputs[:tile], back.astype(wide)], axis=0)
    weight_grad_out = widen(own, out_all)
    weight_grad_qkv, sums_one = widen_qkv(own, q_all, seq_gather(grad_kv_own), w_qkv)
    grad_gain_one = sums_one[:, 0] / gain_attn.astype(wide)
    grad_gain_two = (sums_gate + sums_up)[:, 0] / gain_mlp.astype(wide)
    return (
        layer_out.reshape(tokens.shape),
        grad_inputs.reshape(tokens.shape),
        weight_grad_qkv,
        weight_grad_out,
        weight_grad_gate_up,
        weight_grad_down,
        grad_gain_one,
        grad_gain_two,
    )


def solution(mesh):
    by_token = P("fsdp", "seq", None)
    by_row = P("fsdp", None)
    return jax.shard_map(
        local,
        mesh=mesh,
        in_specs=(by_token, P("fsdp"), by_row, by_row, P("fsdp"), by_row, by_row, by_token),
        out_specs=(by_token, by_token, by_row, by_row, by_row, by_row, P("fsdp"), P("fsdp")),
        check_vma=False,
    )
```

```python
import functools

import jax
import jax.numpy as jnp
from jax import lax
from jax.experimental import pallas as pl
from jax.experimental.pallas import tpu as pltpu
from jax.sharding import PartitionSpec as P

H = 32
KVH = 4
HDIM = 64
FF = 5632
SEQ_LEN = 8192
GROUP = H // KVH

epsilon = 1e-05
low = jnp.bfloat16
wide = jnp.float32


def dot(left, right, left_dim, right_dim):
    return lax.dot_general(
        left, right, (((left_dim,), (right_dim,)), ((), ())), preferred_element_type=wide
    )


def head_columns(ref, chunk, per_chunk):
    return jnp.concatenate(
        [ref[h * HDIM : (h + 1) * HDIM, :] for h in range(chunk * per_chunk, (chunk + 1) * per_chunk)],
        axis=1,
    )


def causal(offset, first, key_block, tile, copies):
    key_places = offset + lax.broadcasted_iota(jnp.int32, (key_block, tile), 0)
    query_places = first + lax.broadcasted_iota(jnp.int32, (key_block, tile), 1)
    return jnp.concatenate([key_places <= query_places] * copies, axis=1)


def each_piece(places, span, tiles, tile, visit):
    own = places[tiles]

    def one(n, _):
        block, rest = n // tiles, n % tiles
        index, half = rest // 2, rest % 2
        sender = jnp.where(half == 0, block, span - 1 - block)
        visit(
            sender,
            pl.multiple_of(((index ^ own) * 2 + half) * tile, tile),
            pl.multiple_of(n * tile, tile),
        )
        return 0

    lax.fori_loop(0, span * tiles, one, 0, unroll=8)


def unpack_kernel(places, kv_ref, keys_ref, values_ref, kt_ref, ones_ref, *, tile, tiles):
    ones_ref[HDIM:, :] = jnp.ones((8, ones_ref.shape[1]), low)

    def visit(sender, start, place):
        piece = kv_ref[sender, :, pl.ds(start, tile)]
        kt_ref[:, pl.ds(place, tile)] = piece[:HDIM]
        ones_ref[:HDIM, pl.ds(place, tile)] = piece[HDIM:]
        turned = piece.astype(wide).T.astype(low)
        keys_ref[pl.ds(place, tile), :] = turned[:, :HDIM]
        values_ref[pl.ds(place, tile), :] = turned[:, HDIM:]

    each_piece(places, kv_ref.shape[0], tiles, tile, visit)


def whole_block(shape):
    return pl.BlockSpec(shape, lambda i, p: (0,) * len(shape))


def unpack(places, kv, tile):
    span, _, slab = kv.shape
    length = span * slab
    shapes = [(length, HDIM), (length, HDIM), (HDIM, length), (HDIM + 8, length)]
    return pl.pallas_call(
        functools.partial(unpack_kernel, tile=tile, tiles=slab // tile),
        grid_spec=pltpu.PrefetchScalarGridSpec(
            num_scalar_prefetch=1,
            grid=(1,),
            in_specs=[whole_block(kv.shape)],
            out_specs=[whole_block(shape) for shape in shapes],
        ),
        out_shape=[jax.ShapeDtypeStruct(shape, low) for shape in shapes],
        compiler_params=pltpu.CompilerParams(vmem_limit_bytes=32 << 20),
        name="unpack",
    )(places, kv)


def attend_kernel(places, q_ref, keys_ref, values_ref, mixed_ref, lse_ref, max_s, sum_s, *, key_block, per_chunk, base):
    tile = q_ref.shape[1]
    chunks = GROUP // per_chunk
    first = places[pl.program_id(0) + base]
    queries = [head_columns(q_ref, c, per_chunk) for c in range(chunks)]
    max_s[...] = jnp.full(max_s.shape, -1e30, wide)
    sum_s[...] = jnp.zeros(sum_s.shape, wide)

    def step(index, masked=0):
        offset = pl.multiple_of(index * key_block, key_block)
        size = masked or key_block
        keys = keys_ref[pl.ds(offset, size), :]
        values = values_ref[:, pl.ds(offset, size)]
        if masked:
            keep = causal(offset, first, size, tile, per_chunk)
        for c in range(chunks):
            scores = jnp.dot(keys, queries[c], preferred_element_type=wide)
            if masked:
                scores = jnp.where(keep, scores, -1e30)
            old = max_s[c]
            new = jnp.maximum(old, jnp.max(scores, axis=0, keepdims=True))
            probs = jnp.exp(scores - new).astype(low)
            max_s[c] = new
            sum_s[c] = sum_s[c] * jnp.exp(old - new) + jnp.dot(
                values, probs, preferred_element_type=wide
            )

    full = first // key_block
    lax.fori_loop(0, full, lambda i, _: (step(i), 0)[1], 0)
    for size in range(tile, key_block + tile, tile):

        @pl.when(first % key_block == size - tile)
        def _(size=size):
            step(full, size)

    for c in range(chunks):
        sums = sum_s[c]
        total = sums[HDIM : HDIM + 1, :]
        mixed = sums[:HDIM, :] * (1.0 / total)
        lse = max_s[c] + jnp.log(total)
        for i in range(per_chunk):
            h = c * per_chunk + i
            mixed_ref[h * HDIM : (h + 1) * HDIM, :] = mixed[:, i * tile : (i + 1) * tile]
            lse_ref[0, h : h + 1, :] = lse[:, i * tile : (i + 1) * tile]


def attend(places, queries, keys, values_ones, tile, base, tiles, key_block=1024, per_chunk=8):
    features, _ = queries.shape
    length = keys.shape[0]
    chunks = GROUP // per_chunk
    pairs = GROUP * tiles * tile * length // 2
    return pl.pallas_call(
        functools.partial(attend_kernel, key_block=key_block, per_chunk=per_chunk, base=base),
        grid_spec=pltpu.PrefetchScalarGridSpec(
            num_scalar_prefetch=1,
            grid=(tiles,),
            in_specs=[
                pl.BlockSpec((features, tile), lambda i, p: (0, i + base)),
                whole_block(keys.shape),
                whole_block(values_ones.shape),
            ],
            out_specs=[
                pl.BlockSpec((features, tile), lambda i, p: (0, i)),
                pl.BlockSpec((1, GROUP, tile), lambda i, p: (i, 0, 0)),
            ],
            scratch_shapes=[
                pltpu.VMEM((chunks, 1, per_chunk * tile), wide),
                pltpu.VMEM((chunks, HDIM + 8, per_chunk * tile), wide),
            ],
        ),
        out_shape=[
            jax.ShapeDtypeStruct((features, tiles * tile), wide),
            jax.ShapeDtypeStruct((tiles, GROUP, tile), wide),
        ],
        compiler_params=pltpu.CompilerParams(vmem_limit_bytes=40 << 20),
        cost_estimate=pl.CostEstimate(
            flops=pairs * HDIM * 16, bytes_accessed=8 << 20, transcendentals=pairs
        ),
        name="attend",
    )(places, queries, keys, values_ones)


def attend_back_kernel(places, *refs, key_block, per_chunk, base, tiles, slab, last):
    q_ref, g_ref, mixed_ref, lse_ref, keys_ref, values_ref, kt_ref = refs[:7]
    if last:
        k_before, v_before, gq_ref, gkv_ref, gq_s, gk_s, gv_s = refs[7:]
    else:
        gq_ref, gk_s, gv_s, gq_s = refs[7:]
    tile = q_ref.shape[1]
    chunks = GROUP // per_chunk
    first = places[pl.program_id(0) + base]

    @pl.when(pl.program_id(0) == 0)
    def _():
        gk_s[...] = k_before[...] if last else jnp.zeros(gk_s.shape, wide)
        gv_s[...] = v_before[...] if last else jnp.zeros(gv_s.shape, wide)

    queries = [head_columns(q_ref, c, per_chunk) for c in range(chunks)]
    grads = [head_columns(g_ref, c, per_chunk) for c in range(chunks)]
    inner = [
        jnp.sum(grads[c].astype(wide) * head_columns(mixed_ref, c, per_chunk), axis=0, keepdims=True)
        for c in range(chunks)
    ]
    lse = [
        jnp.concatenate([lse_ref[0, c * per_chunk + i : c * per_chunk + i + 1, :] for i in range(per_chunk)], axis=1)
        for c in range(chunks)
    ]
    gq_s[...] = jnp.zeros(gq_s.shape, wide)

    def step(index, masked=0):
        offset = pl.multiple_of(index * key_block, key_block)
        size = masked or key_block
        keys = keys_ref[pl.ds(offset, size), :]
        values = values_ref[pl.ds(offset, size), :]
        keys_t = kt_ref[:, pl.ds(offset, size)]
        if masked:
            keep = causal(offset, first, size, tile, per_chunk)
        grad_k = grad_v = None
        for c in range(chunks):
            scores = jnp.dot(keys, queries[c], preferred_element_type=wide)
            if masked:
                scores = jnp.where(keep, scores, -1e30)
            probs = jnp.exp(scores - lse[c])
            grad_probs = jnp.dot(values, grads[c], preferred_element_type=wide)
            grad_scores = (probs * (grad_probs - inner[c])).astype(low)
            more_k = dot(grad_scores, queries[c], 1, 1)
            more_v = dot(probs.astype(low), grads[c], 1, 1)
            gq_s[c] += jnp.dot(keys_t, grad_scores, preferred_element_type=wide)
            grad_k = more_k if grad_k is None else grad_k + more_k
            grad_v = more_v if grad_v is None else grad_v + more_v
        gk_s[pl.ds(offset, size), :] += grad_k
        gv_s[pl.ds(offset, size), :] += grad_v

    full = first // key_block
    lax.fori_loop(0, full, lambda i, _: (step(i), 0)[1], 0)
    for size in range(tile, key_block + tile, tile):

        @pl.when(first % key_block == size - tile)
        def _(size=size):
            step(full, size)

    for c in range(chunks):
        grad_q = gq_s[c] * HDIM**-0.5
        for i in range(per_chunk):
            h = c * per_chunk + i
            gq_ref[h * HDIM : (h + 1) * HDIM, :] = grad_q[:, i * tile : (i + 1) * tile]

    if last:

        @pl.when(pl.program_id(0) == tiles - 1)
        def _():
            def visit(sender, start, place):
                both = jnp.concatenate([gk_s[pl.ds(place, tile), :], gv_s[pl.ds(place, tile), :]], axis=1)
                gkv_ref[sender, :, pl.ds(start, tile)] = both.T.astype(low)

            each_piece(places, gkv_ref.shape[0], slab // tile, tile, visit)


def attend_back(
    places, queries, grads, mixed, lse, keys, values, keys_t, tile, base, tiles, slab, before=None,
    key_block=1024, per_chunk=8,
):
    features, _ = queries.shape
    length = keys.shape[0]
    span = length // slab
    chunks = GROUP // per_chunk
    pairs = GROUP * tiles * tile * length // 2
    last = before is not None
    by_tile = pl.BlockSpec((features, tile), lambda i, p: (0, i))
    packed = (span, 2 * HDIM, slab)
    sums = [pltpu.VMEM((length, HDIM), wide)] * 2
    return pl.pallas_call(
        functools.partial(
            attend_back_kernel,
            key_block=key_block, per_chunk=per_chunk, base=base, tiles=tiles, slab=slab, last=last,
        ),
        grid_spec=pltpu.PrefetchScalarGridSpec(
            num_scalar_prefetch=1,
            grid=(tiles,),
            in_specs=[
                pl.BlockSpec((features, tile), lambda i, p: (0, i + base)),
                by_tile,
                by_tile,
                pl.BlockSpec((1, GROUP, tile), lambda i, p: (i, 0, 0)),
                whole_block(keys.shape),
                whole_block(values.shape),
                whole_block(keys_t.shape),
            ]
            + [whole_block(keys.shape)] * (2 * last),
            out_specs=[by_tile] + ([whole_block(packed)] if last else [whole_block(keys.shape)] * 2),
            scratch_shapes=[pltpu.VMEM((chunks, HDIM, per_chunk * tile), wide)] + sums * last,
        ),
        out_shape=[jax.ShapeDtypeStruct((features, tiles * tile), wide)]
        + ([jax.ShapeDtypeStruct(packed, low)] if last else [jax.ShapeDtypeStruct(keys.shape, wide)] * 2),
        compiler_params=pltpu.CompilerParams(vmem_limit_bytes=56 << 20),
        cost_estimate=pl.CostEstimate(
            flops=pairs * HDIM * 40, bytes_accessed=16 << 20, transcendentals=pairs
        ),
        name="attend_back",
    )(places, queries, grads, mixed, lse, keys, values, keys_t, *(before or ()))


def widen_kernel(own, *refs):
    out_ref = refs[-1]
    for i, ref in enumerate(refs[:-1]):

        @pl.when(pl.program_id(0) == i)
        def _(ref=ref):
            out_ref[...] = ref[...].astype(wide)


def widen(own, pieces):
    parts = len(pieces)
    rows, columns = pieces[0].shape
    return pl.pallas_call(
        widen_kernel,
        grid_spec=pltpu.PrefetchScalarGridSpec(
            num_scalar_prefetch=1,
            grid=(parts,),
            in_specs=[pl.BlockSpec((rows, columns), lambda i, own: (0, 0))] * parts,
            out_specs=pl.BlockSpec((rows, columns), lambda i, own: (0, i ^ own[0])),
        ),
        out_shape=jax.ShapeDtypeStruct((rows, parts * columns), wide),
        compiler_params=pltpu.CompilerParams(vmem_limit_bytes=24 << 20),
        name="widen",
    )(own, *pieces)


def widen_half_kernel(own, *refs, parts):
    weight_ref, (out_ref, total_ref) = refs[parts], refs[-2:]
    step = pl.program_id(0)
    for i, ref in enumerate(refs[:parts]):

        @pl.when(step == i)
        def _(ref=ref):
            value = ref[...].astype(wide)
            out_ref[...] = value
            more = jnp.sum(value * weight_ref[...].astype(wide), axis=1, keepdims=True)
            total_ref[...] = jnp.where(step == 0, more, total_ref[...] + more)


def widen_half(own, pieces, weight, half, before=()):
    parts = len(pieces)
    rows, columns = pieces[0].shape

    def place(i, own):
        return (0, half * parts + (i ^ own[0]))

    return pl.pallas_call(
        functools.partial(widen_half_kernel, parts=parts),
        grid_spec=pltpu.PrefetchScalarGridSpec(
            num_scalar_prefetch=1,
            grid=(parts,),
            in_specs=[pl.BlockSpec((rows, columns), lambda i, own: (0, 0))] * parts
            + [pl.BlockSpec((rows, columns), place)]
            + [pl.BlockSpec(memory_space=pl.ANY)] * len(before),
            out_specs=[
                pl.BlockSpec((rows, columns), place),
                pl.BlockSpec((rows, 1), lambda i, own: (0, 0)),
            ],
        ),
        out_shape=[
            jax.ShapeDtypeStruct((rows, 2 * parts * columns), wide),
            jax.ShapeDtypeStruct((rows, 1), wide),
        ],
        input_output_aliases={parts + 2: 0} if before else {},
        compiler_params=pltpu.CompilerParams(vmem_limit_bytes=32 << 20),
        name="widen_half",
    )(own, *pieces, weight, *before)


def widen_qkv_kernel(own, *refs, parts):
    weight_ref, out_ref, total_ref = refs[-3:]
    step = pl.program_id(0)

    def write(value):
        out_ref[...] = value
        more = jnp.sum(value * weight_ref[...].astype(wide), axis=1, keepdims=True)
        total_ref[...] = jnp.where(step == 0, more, total_ref[...] + more)

    for i, ref in enumerate(refs[:parts]):

        @pl.when(step == i)
        def _(ref=ref):
            write(ref[...].astype(wide))

    @pl.when(step == parts)
    def _():
        pieces = [ref[...].astype(wide) for ref in refs[parts : 2 * parts]]
        ordered = []
        for i in range(parts):
            value = pieces[i]
            for j in range(1, parts):
                value = jnp.where(own[0] == j, pieces[i ^ j], value)
            ordered.append(value)
        write(jnp.concatenate([v[:, :HDIM] for v in ordered] + [v[:, HDIM:] for v in ordered], axis=1))


def widen_qkv(own, queries, rest, weight):
    parts = len(queries)
    rows, columns = queries[0].shape[0], parts * 2 * HDIM

    def place(i, own):
        return (0, jnp.where(i < parts, i ^ own[0], parts))

    return pl.pallas_call(
        functools.partial(widen_qkv_kernel, parts=parts),
        grid_spec=pltpu.PrefetchScalarGridSpec(
            num_scalar_prefetch=1,
            grid=(parts + 1,),
            in_specs=[pl.BlockSpec((rows, columns), lambda i, own: (0, 0))] * parts
            + [pl.BlockSpec((rows, 2 * HDIM), lambda i, own: (0, 0))] * parts
            + [pl.BlockSpec((rows, columns), place)],
            out_specs=[
                pl.BlockSpec((rows, columns), place),
                pl.BlockSpec((rows, 1), lambda i, own: (0, 0)),
            ],
        ),
        out_shape=[
            jax.ShapeDtypeStruct((rows, (parts + 1) * columns), wide),
            jax.ShapeDtypeStruct((rows, 1), wide),
        ],
        compiler_params=pltpu.CompilerParams(vmem_limit_bytes=24 << 20),
        name="widen_qkv",
    )(own, *queries, *rest, weight)


def from_core(value):
    return lax.ppermute(value, "seq", [(i, i ^ 1) for i in range(lax.axis_size("seq"))])


def from_chip(value):
    return lax.ppermute(value, "seq", [(i, i ^ 2) for i in range(lax.axis_size("seq"))])


def seq_gather(value):
    far = from_chip(value)
    return [value, from_core(value), far, from_core(far)]


def seq_sum_core(parts):
    far = parts[2].astype(wide) + from_core(parts[3]).astype(wide)
    near = parts[0].astype(wide) + from_core(parts[1]).astype(wide)
    return near, far.astype(low)


def seq_sum(parts):
    near, far = seq_sum_core(parts)
    return near + from_chip(far).astype(wide)


def slots_by_index(value):
    own = lax.axis_index("seq")
    return [
        lax.dynamic_index_in_dim(value, own ^ j, 0, keepdims=False) for j in range(lax.axis_size("seq"))
    ]


def from_turn(value, by):
    size = lax.axis_size("fsdp")
    return lax.ppermute(value, "fsdp", [(i, (i + 2 * by) % size) for i in range(size)])


def from_pair(value):
    return lax.ppermute(value, "fsdp", [(i, i ^ 1) for i in range(lax.axis_size("fsdp"))])


def team_gather(value):
    half = value.shape[0] // 2
    beside, far = from_pair(value), from_chip(value)
    corner = jnp.concatenate([from_chip(beside[:half]), from_pair(far[half:])], axis=0)
    return [each for held in (value, far, beside, corner) for each in (held, from_core(held))]


def team_sum_core(parts):
    return [
        parts[i].astype(wide) + from_core(parts[i + 1]).astype(wide) for i in range(0, len(parts), 2)
    ]


def team_corner_hops(corner):
    half = corner.shape[0] // 2
    return from_chip(corner[:half]), from_pair(corner[half:])


def team_corner_add(sums, top, bottom):
    near, far, beside, _ = sums
    half = near.shape[0] // 2
    beside = jnp.concatenate([beside[:half] + top.astype(wide), beside[half:]], axis=0)
    far = jnp.concatenate([far[:half], far[half:] + bottom.astype(wide)], axis=0)
    return near, far.astype(low), beside.astype(low)


def team_sum(parts):
    sums = team_sum_core(parts)
    near, far, beside = team_corner_add(sums, *team_corner_hops(sums[3].astype(low)))
    return near + from_chip(far).astype(wide) + from_pair(beside).astype(wide)


def from_diagonal(value):
    return lax.ppermute(value, "seq", [(i, i ^ 3) for i in range(lax.axis_size("seq"))])


def seq_swap(value):
    sent = slots_by_index(value)
    came = [sent[0], from_core(sent[1]), from_chip(sent[2]), from_diagonal(sent[3])]
    return slots_by_index(jnp.stack(came))


def pair_split(value):
    second = lax.axis_index("fsdp") % 2
    axis = value.ndim - 3
    return [lax.dynamic_index_in_dim(value, which, axis, keepdims=False) for which in (second, 1 - second)]


def pair_add(mine, came):
    return (mine.astype(wide) + came.astype(wide)).astype(low)


def turns_sum(pair):
    size = lax.axis_size("fsdp")
    if size != 8:
        teams = [list(range(w, size, 2)) for w in range(2)]
        return lax.psum_scatter(pair, "fsdp", scatter_dimension=0, axis_index_groups=teams)
    index = lax.axis_index("fsdp")

    def part(by):
        return lax.dynamic_index_in_dim(pair, (index // 2 + by) % (size // 2), 0, keepdims=False)

    total = part(0).astype(wide)
    for by in range(1, size // 2):
        total = total + from_turn(part(by), by).astype(wide)
    return total.astype(low)


def turn(vectors, cosine, sine):
    half = HDIM // 2
    first, second = vectors[:, :half], vectors[:, half:]
    return jnp.concatenate([first * cosine - second * sine, second * cosine + first * sine], axis=1)


def norm_back(grad_hat, normal, inverse):
    return inverse * (grad_hat - normal * jnp.mean(grad_hat * normal, axis=-1, keepdims=True))


def inverse_rms(values):
    return lax.rsqrt(jnp.mean(values * values, axis=-1, keepdims=True) + epsilon)


def local(tokens, gain_attn, w_qkv, w_out, gain_mlp, w_gate_up, w_down, cotangent):
    width = tokens.shape[-1]
    seq_parts = lax.axis_size("seq")
    blocks = lax.axis_size("fsdp")
    assert seq_parts == KVH == 4
    own_tokens = tokens.reshape(-1, width)
    rows = own_tokens.shape[0]
    tile = rows // 2
    slab = rows * seq_parts
    span = SEQ_LEN // slab
    seq_index = lax.axis_index("seq")
    position = lax.axis_index("fsdp") % span
    mirrored = span - 1 - position
    sequences = [list(range(i, i + span)) for i in range(0, blocks, span)]
    groups = None if span == blocks else sequences
    width_q = H * HDIM
    width_kv = KVH * HDIM
    q_part = GROUP * HDIM
    ff_part = FF // seq_parts
    ff_own = -(-ff_part // 256) * 128
    ff_shared = 2 * ff_own - ff_part
    second = lax.axis_index("fsdp") % 2
    teams = [list(range(w, blocks, 2)) for w in range(2)]

    def mirror(half):
        pairs = [(g[i], g[span - 1 - i]) for g in sequences for i in range(span)]
        return lax.ppermute(half, "fsdp", pairs)

    def part(weight, start, step, size=None):
        return lax.dynamic_slice_in_dim(weight, start + seq_index * step, size or step, 1)

    def sc_gather(value):
        return lax.all_gather(value, "fsdp", axis=0, tiled=True)

    def ordered(mine, other, axis):
        first = jnp.where(second == 0, mine, other)
        return jnp.concatenate([first, jnp.where(second == 0, other, mine)], axis=axis)

    def ff_rows(weight, start):
        def columns(which):
            return part(weight, start + which * (ff_own - ff_shared), ff_part, ff_own)

        return ordered(columns(second), from_pair(columns(1 - second)), 0)

    def ff_gather(value):
        return lax.all_gather(value, "fsdp", axis=0, tiled=True, axis_index_groups=teams)

    def ff_sum(value):
        return lax.psum_scatter(value, "fsdp", scatter_dimension=0, tiled=True, axis_index_groups=teams)

    def ff_split(value):
        return pair_split(value.reshape(2, -1, value.shape[1]))

    def ff_columns(mine, other):
        left = jnp.where(second == 0, mine, other)
        right = jnp.where(second == 0, other, mine)
        return jnp.concatenate([left, right[:, ff_shared:]], axis=1)

    def ff_keep(value):
        column = lax.broadcasted_iota(jnp.int32, value.shape, 1)
        return jnp.where(column >= second * ff_shared, value, 0.0).astype(low)

    def gather_halves(halves):
        near, far = (seq_gather(half) for half in halves)
        return jnp.stack([jnp.stack(pair) for pair in zip(near, far, strict=True)]).reshape(slab, width)

    def slots(value):
        return value.astype(low).reshape(-1, rows, value.shape[1])

    kept, sent = own_tokens[:tile], own_tokens[tile:]
    halves = [kept, mirror(sent)]
    inputs_low = jnp.concatenate(halves, axis=0)
    own_feed = cotangent.reshape(-1, width)

    gains = jnp.pad(jnp.stack([gain_attn, gain_mlp], axis=1), ((0, 0), (0, 126)))
    first_part = sc_gather(
        jnp.concatenate(
            [
                part(w_qkv, 0, q_part),
                part(w_qkv, width_q, HDIM),
                part(w_qkv, width_q + width_kv, HDIM),
                gains,
                part(w_out, 0, width // seq_parts),
            ],
            axis=1,
        )
    )
    out_columns = first_part[:, -(width // seq_parts) :]
    qkv_part = first_part[:, : q_part + 2 * HDIM]
    gain_one = first_part[:, q_part + 2 * HDIM].astype(wide)
    gain_two = first_part[:, q_part + 2 * HDIM + 1].astype(wide)

    all_inputs = gather_halves(halves).astype(wide)
    normed_one = lax.optimization_barrier((all_inputs * inverse_rms(all_inputs) * gain_one).astype(low))
    projected = dot(qkv_part, normed_one, 0, 1)
    frequency = 1.0 / 10000.0 ** (jnp.arange(HDIM // 2, dtype=wide) * (2.0 / HDIM))
    row = jnp.arange(slab, dtype=jnp.int32)
    within = (row // rows ^ seq_index) * rows + row % rows
    row_places = jnp.where(row % rows < tile, position, mirrored) * slab + within
    angles = frequency[:, None] * row_places.astype(wide)[None, :]
    cosine, sine = jnp.cos(angles), jnp.sin(angles)
    places = jnp.concatenate([row_places[::tile], seq_index[None].astype(jnp.int32)])
    queries = turn(projected[:q_part].reshape(GROUP, HDIM, slab), cosine, sine) * HDIM**-0.5
    queries = queries.reshape(q_part, slab).astype(low)
    keys_own = turn(projected[q_part : q_part + HDIM].reshape(1, HDIM, slab), cosine, sine)[0]
    kv_own = jnp.concatenate([keys_own, projected[q_part + HDIM :]], axis=0).astype(low)

    kv_own, own_feed, w_gate, w_up, w_down, out_columns = lax.optimization_barrier(
        (kv_own, own_feed, w_gate_up, w_gate_up, w_down, out_columns)
    )
    kv = lax.all_gather(kv_own, "fsdp", axis_index_groups=groups)
    grad_feed_low = jnp.concatenate([own_feed[:tile], mirror(own_feed[tile:])], axis=0)
    out_part = seq_swap(out_columns.reshape(seq_parts, -1, width // seq_parts))
    gate_own, up_own, down_own = ff_rows(w_gate, 0), ff_rows(w_up, FF), ff_rows(w_down, 0)
    gate_own, up_own, down_own, kv, queries, grad_feed_low, out_part = lax.optimization_barrier(
        (gate_own, up_own, down_own, kv, queries, grad_feed_low, out_part)
    )
    out_part = jnp.concatenate(out_part, axis=1)
    gate_part, up_part, down_part = ff_gather(gate_own), ff_gather(up_own), ff_gather(down_own)
    keys, values, keys_t, values_ones = unpack(places, kv, tile)

    tiles = slab // tile // 2
    feed_beside, feed_far = from_pair(grad_feed_low), from_chip(grad_feed_low)
    mixed_far, lse_far = attend(places, queries, keys, values_ones, tile, tiles, tiles)
    mixed_far, feed_beside, feed_far = lax.optimization_barrier((mixed_far, feed_beside, feed_far))
    part_two, part_three = slots(dot(mixed_far.astype(low), out_part, 0, 0))
    branch_far = (part_two.astype(wide) + from_core(part_three).astype(wide)).astype(low)
    branch_far, queries = lax.optimization_barrier((branch_far, queries))
    branch_came = from_chip(branch_far)
    feed_corner = [from_chip(feed_beside[:tile]), from_pair(feed_far[tile:])]
    mixed_near, lse_near = attend(places, queries, keys, values_ones, tile, 0, tiles)
    mixed_near, branch_came, feed_corner = lax.optimization_barrier((mixed_near, branch_came, feed_corner))
    feed_corner = jnp.concatenate(feed_corner, axis=0)
    part_zero, part_one = slots(dot(mixed_near.astype(low), out_part, 0, 0))
    inputs = inputs_low.astype(wide)
    middle = inputs + (
        part_zero.astype(wide) + from_core(part_one).astype(wide) + branch_came.astype(wide)
    )
    inverse_two = inverse_rms(middle)
    hat_two = middle * inverse_two
    normed_two = jnp.concatenate(team_gather((hat_two * gain_two).astype(low)), axis=0)
    grad_feed = jnp.concatenate(
        [each for held in (grad_feed_low, feed_far, feed_beside, feed_corner) for each in (held, from_core(held))],
        axis=0,
    )
    normed_two, grad_feed = lax.optimization_barrier((normed_two, grad_feed))

    gate = jnp.dot(normed_two, gate_part, preferred_element_type=wide)
    up = jnp.dot(normed_two, up_part, preferred_element_type=wide)
    sigmoid = jax.nn.sigmoid(gate)
    silu = gate * sigmoid
    hidden = ff_keep(silu * up)
    grad_hidden = jnp.dot(grad_feed, down_part, preferred_element_type=wide)
    grad_gate = ff_keep(grad_hidden * up * sigmoid * (1.0 + gate * (1.0 - sigmoid)))
    grad_up = ff_keep(grad_hidden * silu)
    product_two = (dot(grad_gate, gate_part, 1, 1) + dot(grad_up, up_part, 1, 1)).astype(low)
    product_two, hidden, grad_gate, grad_up = lax.optimization_barrier(
        (product_two, hidden, grad_gate, grad_up)
    )
    local_down = dot(grad_feed, hidden, 0, 0).astype(low)
    local_gate = dot(normed_two, grad_gate, 0, 0).astype(low)
    local_up = dot(normed_two, grad_up, 0, 0).astype(low)
    feed_sums = team_sum_core(slots(dot(hidden, down_part, 1, 1)))
    grad_normed_two = team_sum(slots(product_two))
    grad_middle = grad_feed_low.astype(wide) + norm_back(
        grad_normed_two * gain_two, hat_two, inverse_two
    )
    sum_down = ff_sum(local_down)
    branch_low, feed_sums, sum_down, local_gate, local_up = lax.optimization_barrier(
        (grad_middle.astype(low), feed_sums, sum_down, local_gate, local_up)
    )
    sum_gate, sum_up = ff_sum(local_gate), ff_sum(local_up)

    back_near = jnp.concatenate([branch_low, from_core(branch_low)], axis=0)
    grads_near = dot(out_part, back_near, 1, 1).astype(low)
    back_come = from_chip(branch_low)
    feed_hops = team_corner_hops(feed_sums[3].astype(low))
    mine_down, theirs = ff_split(sum_down)
    other_down = from_pair(theirs)
    grad_q_near, grad_k, grad_v = attend_back(
        places, queries, grads_near, mixed_near, lse_near, keys, values, keys_t, tile, 0, tiles, slab
    )
    grad_q_near, grad_k, grad_v, back_come, feed_hops, other_down, sum_gate = lax.optimization_barrier(
        (grad_q_near, grad_k, grad_v, back_come, feed_hops, other_down, sum_gate)
    )
    feed_near, feed_far, feed_beside = team_corner_add(feed_sums, *feed_hops)
    own_down = ff_columns(mine_down, other_down)
    mine_gate, theirs_gate = ff_split(sum_gate)
    back_far = jnp.concatenate([back_come, from_core(back_come)], axis=0)
    grads_far = dot(out_part, back_far, 1, 1).astype(low)
    local_out = (
        dot(mixed_near.astype(low), back_near, 1, 0) + dot(mixed_far.astype(low), back_far, 1, 0)
    ).astype(low)
    mine_out, theirs_out = pair_split(local_out.reshape(blocks // 8, 2, -1, width))
    grads_far, theirs_out, feed_far, feed_beside, own_down, theirs_gate = lax.optimization_barrier(
        (grads_far, theirs_out, feed_far, feed_beside, own_down, theirs_gate)
    )
    other_out = from_pair(theirs_out)
    feed_far, feed_beside = from_chip(feed_far), from_pair(feed_beside)
    far_down = from_chip(own_down)
    other_gate = from_pair(theirs_gate)
    grad_q_far, grad_kv = attend_back(
        places, queries, grads_far, mixed_far, lse_far, keys, values, keys_t, tile, tiles, tiles, slab,
        before=(grad_k, grad_v),
    )
    grad_q_far, grad_kv, feed_far, feed_beside, far_down, other_gate, other_out, sum_up = lax.optimization_barrier(
        (grad_q_far, grad_kv, feed_far, feed_beside, far_down, other_gate, other_out, sum_up)
    )
    layer_out = (middle + feed_near + feed_far.astype(wide) + feed_beside.astype(wide)).astype(low)

    grad_kv = lax.psum_scatter(grad_kv, "fsdp", scatter_dimension=0, axis_index_groups=groups)
    grad_q = jnp.concatenate([grad_q_near, grad_q_far], axis=1).astype(low).astype(wide)
    grad_q = turn(grad_q.reshape(GROUP, HDIM, slab), cosine, -sine).reshape(q_part, slab).astype(low)
    own = seq_index[None].astype(jnp.int32)
    mine_q, theirs = pair_split(dot(normed_one, grad_q, 0, 1).astype(low).reshape(blocks // 2, 2, -1, q_part))
    other_q = from_pair(theirs)
    out_pair = pair_add(mine_out, other_out).reshape(-1, seq_parts, width // seq_parts)
    out_sums = seq_swap(out_pair.transpose(1, 0, 2))
    down_all = [own_down, from_core(own_down), far_down, from_core(far_down)]
    gate_all = seq_gather(ff_columns(mine_gate, other_gate))
    mine, theirs = ff_split(sum_up)
    up_all = seq_gather(ff_columns(mine, from_pair(theirs)))
    q_far = dot(grad_q[:, slab // 2 :], qkv_part[:, :q_part], 0, 1)
    q_near = dot(grad_q[:, : slab // 2], qkv_part[:, :q_part], 0, 1)
    sent_out = layer_out[tile:]
    grad_kv, other_q, out_sums, down_all, gate_all, up_all, sent_out, q_far, q_near = lax.optimization_barrier(
        (grad_kv, other_q, out_sums, down_all, gate_all, up_all, sent_out, q_far, q_near)
    )
    grad_k = turn(grad_kv[:HDIM].astype(wide).reshape(1, HDIM, slab), cosine, -sine)[0].astype(low)
    grad_kv = jnp.concatenate([grad_k, grad_kv[HDIM:]], axis=0)
    part_two, part_three = slots(q_far + dot(grad_kv[:, slab // 2 :], qkv_part[:, q_part:], 0, 1))
    far_one = (part_two.astype(wide) + from_core(part_three).astype(wide)).astype(low)
    far_one, grad_kv, q_near, mine_q, other_q, out_sums = lax.optimization_barrier(
        (far_one, grad_kv, q_near, mine_q, other_q, out_sums)
    )
    came_one = from_chip(far_one)
    grad_out_own = ff_sum(jnp.concatenate(out_sums, axis=0))
    grad_q_own = ff_sum(pair_add(mine_q, other_q).reshape(-1, q_part))
    part_zero, part_one = slots(q_near + dot(grad_kv[:, : slab // 2], qkv_part[:, q_part:], 0, 1))
    weight_grad_down = widen(own, down_all)
    weight_grad_gate, sums_gate = widen_half(own, gate_all, w_gate_up, 0)
    weight_grad_gate_up, sums_up = widen_half(own, up_all, w_gate_up, 1, (weight_grad_gate,))
    mine_kv, theirs = pair_split(
        dot(normed_one, grad_kv, 0, 1).astype(low).reshape(blocks // 2, 2, -1, 2 * HDIM)
    )
    other_kv = from_pair(theirs)
    near_one = part_zero.astype(wide) + from_core(part_one).astype(wide)
    near_one, came_one, other_kv = lax.optimization_barrier((near_one, came_one, other_kv))

    grad_normed_one = near_one + came_one.astype(wide)
    inverse_one = inverse_rms(inputs)
    grad_inputs = grad_middle + norm_back(
        grad_normed_one * gain_one, inputs * inverse_one, inverse_one
    )
    grad_inputs, kv_pair = lax.optimization_barrier((grad_inputs, pair_add(mine_kv, other_kv)))
    back = mirror(grad_inputs[tile:].astype(low))
    grad_kv_own = turns_sum(kv_pair)
    back, grad_kv_own, grad_q_own, grad_out_own, sent_out, weight_grad_gate_up, weight_grad_down = (
        lax.optimization_barrier(
            (back, grad_kv_own, grad_q_own, grad_out_own, sent_out, weight_grad_gate_up, weight_grad_down)
        )
    )
    layer_out = jnp.concatenate([layer_out[:tile], mirror(sent_out)], axis=0)
    q_all, out_all = seq_gather(grad_q_own), seq_gather(grad_out_own)
    grad_inputs = jnp.concatenate([grad_inputs[:tile], back.astype(wide)], axis=0)
    weight_grad_out = widen(own, out_all)
    weight_grad_qkv, sums_one = widen_qkv(own, q_all, seq_gather(grad_kv_own), w_qkv)
    grad_gain_one = sums_one[:, 0] / gain_attn.astype(wide)
    grad_gain_two = (sums_gate + sums_up)[:, 0] / gain_mlp.astype(wide)
    return (
        layer_out.reshape(tokens.shape),
        grad_inputs.reshape(tokens.shape),
        weight_grad_qkv,
        weight_grad_out,
        weight_grad_gate_up,
        weight_grad_down,
        grad_gain_one,
        grad_gain_two,
    )


def solution(mesh):
    by_token = P("fsdp", "seq", None)
    by_row = P("fsdp", None)
    return jax.shard_map(
        local,
        mesh=mesh,
        in_specs=(by_token, P("fsdp"), by_row, by_row, P("fsdp"), by_row, by_row, by_token),
        out_specs=(by_token, by_token, by_row, by_row, by_row, by_row, P("fsdp"), P("fsdp")),
        check_vma=False,
    )
```
